128 devices in a mesh: dp: 32 (over x, z, core), owner: 4 (over y).
Axes of the slice: x: 4, y: 4, z: 4, core: 2. Of those that a mesh axis runs over, the one named last changes fastest.
Arguments:
- hidden: bfloat16 [32768, 6912], P(('dp', 'owner')), may hold values from -6 to 6
- grad_out: bfloat16 [32768, 2560], P(('dp', 'owner')), may hold values from -6 to 6
- block_list: int32 [512, 2], replicated, may hold values from 0 to 107, as said below
- live_block_count: int32 [128], replicated, may hold values from 1 to 4, as said below
- master: float32 [512, 4096], P(('dp', 'owner')), may hold values from -6 to 6
- moment: float32 [512, 4096], P(('dp', 'owner')), may hold values from -6 to 6
- variance: float32 [512, 4096], P(('dp', 'owner')), may hold values from 0.25 to 4
Outputs:
- new_master: float32 [512, 4096], P(('dp', 'owner'))
- new_moment: float32 [512, 4096], P(('dp', 'owner'))
- new_variance: float32 [512, 4096], P(('dp', 'owner'))
- clipped_grad: float32 [512, 4096], P(('dp', 'owner'))
- published: bfloat16 [512, 4096], replicated
The draws below stay inside these ranges and needn't reach their ends.
Inputs may be any that keep to these rules, and one draw needn't show every extreme that they name: `block_list`: each row names a block: its row index below 108, its column index below 40; all rows name different blocks. Rows 4 o to 4 o + 3 are owner o's slots; owner o is the device whose index along dp is o // 4 and whose index along the mesh axis `owner` is o mod 4. Owner o's first live_block_count[o] slots are live, the rest padding; some owner's slots are all live.
All inputs are finite; a program needn't handle non-finite values.
Results may differ from the reference program's by a relative error of at most 0.001.
Values may be sent and summed in bfloat16 or wider, within the bound.
A program may use at most 128 MiB of HBM per device.

```python
import math
import jax
import jax.numpy as jnp
from jax import lax

D_WIN = 2560
FF_WIN = 6912
BLOCK_SIDE_SIZE = 64
OWNER_SLOTS = 4
OWNERS = 128
TOTAL_SLOTS = 512
TOKENS = 32768


def draw_block_list(key, part):
    key = jax.random.fold_in(key, 11)
    across = D_WIN // BLOCK_SIDE_SIZE
    all_block_list = FF_WIN // BLOCK_SIDE_SIZE * across
    picked_slots = jax.random.permutation(key, all_block_list)[:TOTAL_SLOTS].astype(jnp.int32)
    return jnp.stack([picked_slots // across, picked_slots % across], axis=1).astype(jnp.int32)


def draw_live_block_count(key, part):
    key = jax.random.fold_in(key, 23)
    first_key, second_key = jax.random.split(key)
    counts = jax.random.randint(first_key, (OWNERS,), max(1, OWNER_SLOTS // 4), OWNER_SLOTS + 1)
    full_owner = jax.random.randint(second_key, (), 0, OWNERS)
    return jnp.where(jnp.arange(OWNERS) == full_owner, OWNER_SLOTS, counts).astype(jnp.int32)


def block_scale(key, extent, cuts, smallest, largest):
    level = 1.0
    for position, shards_of in cuts:
        heights = jax.random.uniform(jax.random.fold_in(jax.random.fold_in(key, 6), position), (shards_of,), jnp.float32, smallest / len(cuts), largest / len(cuts))
        level = level * jnp.repeat(jnp.exp(heights), extent[position] // shards_of).reshape((-1,) + (1,) * (len(extent) - 1 - position))
    return level


def scatter_about(rng, extent, scale, most, cuts=(), held_as=jnp.bfloat16):
    loudness = block_scale(rng, extent, cuts, -0.22, 0.18) if cuts else 1.0
    drawn = jax.random.normal(rng, extent, jnp.float32) * scale * loudness
    return jnp.minimum(jnp.maximum(drawn, -most), most).astype(held_as)


def setup_inputs(seed: int = 0) -> dict:
    arg_keys = jax.random.split(jax.random.key(seed), 8)
    hidden = scatter_about(arg_keys[0], (TOKENS, FF_WIN), 1.0, 6.0, ((0, 128),))
    grad_out = scatter_about(arg_keys[1], (TOKENS, D_WIN), 1.0, 6.0, ((0, 128),))
    block_list = draw_block_list(jax.random.fold_in(arg_keys[7], 71), 0)
    live_block_count = draw_live_block_count(jax.random.fold_in(arg_keys[7], 71), 0)
    master = scatter_about(arg_keys[4], (TOTAL_SLOTS, BLOCK_SIDE_SIZE * BLOCK_SIDE_SIZE), 1.0, 6.0, ((0, 128),), jnp.float32)
    moment = scatter_about(arg_keys[5], (TOTAL_SLOTS, BLOCK_SIDE_SIZE * BLOCK_SIDE_SIZE), 0.5, 6.0, ((0, 128),), jnp.float32)
    variance = jnp.clip(jnp.exp(math.log(4.0) - 2.7725887 * jax.random.uniform(arg_keys[6], (TOTAL_SLOTS, BLOCK_SIDE_SIZE * BLOCK_SIDE_SIZE), jnp.float32) ** block_scale(arg_keys[6], (TOTAL_SLOTS, BLOCK_SIDE_SIZE * BLOCK_SIDE_SIZE), ((0, 128),), -0.2, 0.2)), 0.25, 4.0)
    return dict(hidden=hidden, grad_out=grad_out, block_list=block_list, live_block_count=live_block_count, master=master, moment=moment, variance=variance)


def reference(hidden, grad_out, block_list, live_block_count, master, moment, variance):
    offsets = jnp.arange(BLOCK_SIDE_SIZE, dtype=jnp.int32)
    row_indices = block_list[:, 0].reshape(OWNERS, OWNER_SLOTS)
    column_indices = block_list[:, 1].reshape(OWNERS, OWNER_SLOTS)

    def owned_block_grad(id_pair):
        row_sel, col_sel = id_pair
        row_index = (row_sel[:, None] * BLOCK_SIDE_SIZE + offsets[None, :]).reshape(-1).astype(jnp.int32)
        col_index = (col_sel[:, None] * BLOCK_SIDE_SIZE + offsets[None, :]).reshape(-1).astype(jnp.int32)
        left_cols = jnp.take(hidden, row_index, axis=1).astype(jnp.float32).reshape(TOKENS, OWNER_SLOTS, BLOCK_SIDE_SIZE)
        right_cols = jnp.take(grad_out, col_index, axis=1).astype(jnp.float32).reshape(TOKENS, OWNER_SLOTS, BLOCK_SIDE_SIZE)
        return jnp.einsum('tsa,tsb->sab', left_cols, right_cols).reshape(OWNER_SLOTS, BLOCK_SIDE_SIZE * BLOCK_SIDE_SIZE)
    weight_gradient = lax.map(owned_block_grad, (row_indices, column_indices)).reshape(TOTAL_SLOTS, BLOCK_SIDE_SIZE * BLOCK_SIDE_SIZE)
    active_slot_mask = (jnp.arange(OWNER_SLOTS, dtype=jnp.int32)[None, :] < live_block_count[:, None]).reshape(TOTAL_SLOTS, 1)
    weight_gradient = jnp.where(active_slot_mask, weight_gradient, jnp.zeros_like(weight_gradient))
    live_total = jnp.sum(live_block_count).astype(jnp.float32) * (BLOCK_SIDE_SIZE * BLOCK_SIDE_SIZE)
    mean_square = jnp.sum(weight_gradient * weight_gradient) / live_total
    clip_scale = jnp.minimum(1.0, 1.0 / jnp.sqrt(mean_square + 1e-06))
    clipped_grad = clip_scale * weight_gradient
    new_moment = 0.9 * moment + 0.1 * clipped_grad
    new_variance = 0.95 * variance + 0.05 * clipped_grad * clipped_grad
    moment_hat = new_moment / (1.0 - 0.9 ** 20)
    variance_hat = new_variance / (1.0 - 0.95 ** 20)
    new_master = master - 0.02 * (moment_hat / (jnp.sqrt(variance_hat) + 1e-08) + 0.1 * master)
    published = new_master.astype(jnp.bfloat16)
    return (new_master, new_moment, new_variance, clipped_grad, published)
```

```python
import functools

import jax
import jax.numpy as jnp
from jax import lax
from jax.experimental import pallas as pl
from jax.experimental.pallas import tpu as pltpu
from jax.sharding import PartitionSpec as P

MESH = pl.DeviceIdType.MESH
SIDE = 64
TOKENS = 256
SLAB_ORDER = (2, 1, 3, 0)
STREAMS = ((0, 48, "xyz"), (48, 48, "yzx"), (96, 32, "zxy"))
F32 = jnp.float32


def where_am_i():
    dp = lax.axis_index("dp")
    y = lax.axis_index("owner")
    return {"x": dp // 8, "z": (dp // 2) % 4, "c": dp % 2, "y": y}


def device_at(place):
    return ((place["x"] * 4 + place["z"]) * 2 + place["c"], place["y"])


def moved(me, **by):
    place = dict(me)
    for axis, step in by.items():
        place[axis] = (me[axis] + step) % (2 if axis == "c" else 4)
    return place


def exponent_of(top):
    top = jnp.maximum(jnp.full((16, 128), jnp.max(top), F32), 1e-30)
    return jnp.ceil(jnp.log2(top * (1.0 / 32000.0)))


def encode(values, inverse):
    return jnp.round(values * inverse).astype(jnp.int32).astype(jnp.int16)


def splat(tile):
    return tile[0:1, :].astype(F32)


def region(buf, stream, level, me, fixed):
    first, rows, _ = stream
    index = [fixed.get(a, slice(None)) for a in "xzcy"]
    return buf.at[(*index, pl.ds(first, rows), slice(None))]


def kernel(
    list_ref, hidden_hbm, grad_out_hbm, live_ref, master_ref, moment_ref, variance_ref,
    new_master_ref, new_moment_ref, new_variance_ref, clipped_ref, published,
    hidden, grad_out, grad_out_t, acc, pair_part, sib_send, sib_recv,
    send1a, recv1a, send1b, recv1b, send1c, recv1c,
    send2a, recv2a, send2b, recv2b, send2c, recv2c,
    send3a, recv3a, send3b, recv3b, send3c, recv3c,
    turned, flat, sum_send, sum_recv,
    load_sem, send_sem, recv_sem,
):
    me = where_am_i()
    px, py, pz, pc = me["x"], me["y"], me["z"], me["c"]
    loads = [
        pltpu.make_async_copy(grad_out_hbm, grad_out, load_sem.at[0]),
        pltpu.make_async_copy(hidden_hbm, hidden, load_sem.at[1]),
    ]
    for load in loads:
        load.start()

    peers = [moved(me, c=1)]
    peers += [moved(me, **{a: d}) for a in "xyz" for d in (1, 2, 3)]
    peers += [moved(me, x=d, c=1) for d in (1, 2, 3)]
    peers += [moved(me, y=i, z=j) for i in (1, 2, 3) for j in (1, 2, 3)]
    barrier = pltpu.get_barrier_semaphore()
    for peer in peers:
        pl.semaphore_signal(barrier, inc=1, device_id=device_at(peer), device_id_type=MESH)

    loads[0].wait()
    for t in range(20):
        grad_out_t[pl.ds(t * 128, 128), :] = grad_out[:, t * 128 : (t + 1) * 128].T
    loads[1].wait()
    pl.semaphore_wait(barrier, len(peers))

    issued = []

    def send(src, dst, to):
        n = len(issued)
        copy = pltpu.make_async_remote_copy(
            src_ref=src, dst_ref=dst, send_sem=send_sem.at[n], recv_sem=recv_sem.at[n],
            device_id=device_at(to), device_id_type=MESH,
        )
        copy.start()
        issued.append(copy)
        return copy

    lane = lax.broadcasted_iota(jnp.int32, (SIDE, 128), 1)

    low = lane < SIDE

    def two_blocks(pair):
        both, odd = [], []
        for slot in (2 * pair, 2 * pair + 1):
            row, column = list_ref[2 * slot], list_ref[2 * slot + 1]
            left = grad_out_t[pl.ds(column * SIDE, SIDE), :]
            right = hidden[:, pl.ds((row >> 1) * 128, 128)]
            both.append(jnp.dot(left, right, preferred_element_type=F32))
            odd.append(row & 1)
        crossed = pltpu.roll(jnp.where(low, both[1], both[0]), SIDE, 1)
        straight = jnp.where(low, both[0], both[1])
        return jnp.where(jnp.where(low, odd[0], 1 - odd[1]) == 1, crossed, straight)

    sends1 = []
    for k, step in enumerate(SLAB_ORDER):
        zk = (pz + step) % 4

        def for_sibling(i, top, zk=zk):
            for u in range(16):
                x, y, p = 2 * i + u // 8, (u // 2) % 4, u % 2
                owner = ((x * 4 + zk) * 2 + (1 - pc)) * 4 + y
                part = two_blocks(2 * owner + p)
                pair_part[x, y, pl.ds(p * SIDE, SIDE), :] = part
                top = jnp.maximum(top, jnp.max(jnp.abs(part).reshape(8, 8, 128), axis=0))
            return top

        top = lax.fori_loop(0, 2, for_sibling, jnp.zeros((8, 128), F32))
        exponent = exponent_of(top)
        inverse = jnp.exp2(-exponent)[0:1, :]
        for x in range(4):
            for y in range(4):
                sib_send[k, pl.ds((x * 4 + y) * 128, 128), :] = encode(pair_part[x, y], inverse)
        sib_send[k, pl.ds(2048, 16), :] = exponent.astype(jnp.int32).astype(jnp.int16)
        sib = send(sib_send.at[k], sib_recv.at[k], moved(me, c=1))

        def for_self(i, carry, zk=zk):
            for u in range(16):
                x, y, p = 2 * i + u // 8, (u // 2) % 4, u % 2
                owner = ((x * 4 + zk) * 2 + pc) * 4 + y
                acc[x, zk, y, pl.ds(p * SIDE, SIDE), :] = two_blocks(2 * owner + p)
            return carry

        lax.fori_loop(0, 2, for_self, 0)
        sib.wait_recv()
        scale = jnp.exp2(splat(sib_recv[k, pl.ds(2048, 16), :]))
        top = jnp.zeros((8, 128), F32)
        for x in range(4):
            for y in range(4):
                total = acc[x, zk, y] + scale * sib_recv[k, pl.ds((x * 4 + y) * 128, 128), :].astype(F32)
                acc[x, zk, y] = total
                top = jnp.maximum(top, jnp.max(jnp.abs(total).reshape(16, 8, 128), axis=0))
        exponent = exponent_of(top)
        inverse = jnp.exp2(-exponent)[0:1, :]
        exponent = exponent.astype(jnp.int32).astype(jnp.int16)
        slab = []
        if step:
            for x in range(4):
                for y in range(4):
                    send1c[step - 1, pl.ds((x * 4 + y) * 32, 32), :] = encode(acc[x, zk, y, 96:128, :], inverse)
            send1c[step - 1, pl.ds(512, 16), :] = exponent
            slab.append(send(send1c.at[step - 1], recv1c.at[step - 1], moved(me, z=step)))
        for d in (2, 1, 3):
            to = (px + d) % 4
            for y in range(4):
                send1a[k, d - 1, pl.ds(y * 48, 48), :] = encode(acc[to, zk, y, 0:48, :], inverse)
            send1a[k, d - 1, pl.ds(192, 16), :] = exponent
            slab.append(send(send1a.at[k, d - 1], recv1a.at[k, d - 1], moved(me, x=d)))
            to = (py + d) % 4
            for x in range(4):
                send1b[k, d - 1, pl.ds(x * 48, 48), :] = encode(acc[x, zk, to, 48:96, :], inverse)
            send1b[k, d - 1, pl.ds(192, 16), :] = exponent
            slab.append(send(send1b.at[k, d - 1], recv1b.at[k, d - 1], moved(me, y=d)))
        sends1.append(slab)

    def finish(k):
        step = SLAB_ORDER[k]
        zk = (pz + step) % 4
        slab = list(sends1[k])
        if step:
            slab.pop(0).wait_recv()
            scale = jnp.exp2(splat(recv1c[step - 1, pl.ds(512, 16), :]))
            for x in range(4):
                for y in range(4):
                    acc[x, pz, y, 96:128, :] += scale * recv1c[step - 1, pl.ds((x * 4 + y) * 32, 32), :].astype(F32)
        for n, d in enumerate((2, 1, 3)):
            slab[2 * n].wait_recv()
            scale = jnp.exp2(splat(recv1a[k, d - 1, pl.ds(192, 16), :]))
            for y in range(4):
                acc[px, zk, y, 0:48, :] += scale * recv1a[k, d - 1, pl.ds(y * 48, 48), :].astype(F32)
            slab[2 * n + 1].wait_recv()
            scale = jnp.exp2(splat(recv1b[k, d - 1, pl.ds(192, 16), :]))
            for x in range(4):
                acc[x, zk, py, 48:96, :] += scale * recv1b[k, d - 1, pl.ds(x * 48, 48), :].astype(F32)

    for k in range(4):
        finish(k)

    def later_phase(axis, out_buf, in_buf, rows, first, count, place):
        held = [[acc[(*place(j, (me[axis] + d) % 4), pl.ds(first, rows), slice(None))] for j in range(count)] for d in (2, 1, 3)]
        top = functools.reduce(jnp.maximum, [jnp.max(jnp.abs(v).reshape(rows // 8, 8, 128), axis=0) for h in held for v in h])
        exponent = exponent_of(top)
        inverse = jnp.exp2(-exponent)[0:1, :]
        exponent = exponent.astype(jnp.int32).astype(jnp.int16)
        copies = []
        for h, d in zip(held, (2, 1, 3), strict=True):
            for j, v in enumerate(h):
                out_buf[d - 1, pl.ds(j * rows, rows), :] = encode(v, inverse)
            out_buf[d - 1, pl.ds(count * rows, 16), :] = exponent
            copies.append(send(out_buf.at[d - 1], in_buf.at[d - 1], moved(me, **{axis: d})))

        def add():
            for d, copy in zip((2, 1, 3), copies, strict=True):
                copy.wait_recv()
                scale = jnp.exp2(splat(in_buf[d - 1, pl.ds(count * rows, 16), :]))
                for j in range(count):
                    acc[(*place(j, me[axis]), pl.ds(first, rows), slice(None))] += scale * in_buf[d - 1, pl.ds(j * rows, rows), :].astype(F32)

        return add

    adds = [
        later_phase("x", send2c, recv2c, 32, 96, 4, lambda j, q: (q, pz, j)),
        later_phase("y", send2a, recv2a, 48, 0, 4, lambda j, q: (px, j, q)),
        later_phase("z", send2b, recv2b, 48, 48, 4, lambda j, q: (j, q, py)),
    ]
    adds[0]()
    last = [later_phase("y", send3c, recv3c, 32, 96, 1, lambda j, q: (px, pz, q))]
    adds[1]()
    last.append(later_phase("z", send3a, recv3a, 48, 0, 1, lambda j, q: (px, q, py)))
    adds[2]()
    last.append(later_phase("x", send3b, recv3b, 48, 48, 1, lambda j, q: (q, pz, py)))
    for add in last:
        add()

    counts = live_ref[0:1, :]
    owner = ((px * 4 + pz) * 2 + pc) * 4 + py
    at = lax.broadcasted_iota(jnp.int32, (1, 128), 1)
    mine = jnp.sum(jnp.where(at == owner, counts, 0.0))
    live_total = jnp.sum(counts) * float(SIDE * SIDE)
    slot = 2 * (lax.broadcasted_iota(jnp.int32, (128, 128), 0) // SIDE) + lax.broadcasted_iota(jnp.int32, (128, 128), 1) // SIDE
    own = jnp.where(slot.astype(F32) < mine, acc[px, pz, py], 0.0)
    sum_send[0] = jnp.full((8, 128), jnp.sum(own * own), F32)
    copies = []
    for n, by in enumerate([{"c": 1}] + [{"x": d, "c": c} for d in (1, 2, 3) for c in (0, 1)]):
        copies.append(send(sum_send.at[0], sum_recv.at[n], moved(me, **by)))
    turned[...] = own.T
    even, odd = turned[pl.ds(0, SIDE, 2), :], turned[pl.ds(1, SIDE, 2), :]
    flat[pl.ds(0, SIDE), :] = jnp.where(lane < SIDE, even, pltpu.roll(odd, SIDE, 1))
    flat[pl.ds(SIDE, SIDE), :] = jnp.where(lane < SIDE, pltpu.roll(even, SIDE, 1), odd)
    square = sum_send[0]
    for n, copy in enumerate(copies):
        copy.wait_recv()
        square += sum_recv[n]
    sum_send[1] = square
    copies = []
    for i in range(4):
        for j in range(4):
            if i or j:
                copies.append(send(sum_send.at[1], sum_recv.at[7 + len(copies)], moved(me, y=i, z=j)))
    for n, copy in enumerate(copies):
        copy.wait_recv()
        square += sum_recv[7 + n]
    mean_square = square[0:4] / live_total
    clip = jnp.minimum(1.0, 1.0 / jnp.sqrt(mean_square + 1e-06))

    for t in range(32):
        at = pl.ds(t * 128, 128)
        clipped = clip * flat[pl.ds(t, 4, 32), :]
        new_moment = 0.9 * moment_ref[:, at] + 0.1 * clipped
        new_variance = 0.95 * variance_ref[:, at] + 0.05 * clipped * clipped
        moment_hat = new_moment / (1.0 - 0.9**20)
        variance_hat = new_variance / (1.0 - 0.95**20)
        master = master_ref[:, at]
        new_master = master - 0.02 * (moment_hat / (jnp.sqrt(variance_hat) + 1e-08) + 0.1 * master)
        clipped_ref[:, at] = clipped
        new_moment_ref[:, at] = new_moment
        new_variance_ref[:, at] = new_variance
        new_master_ref[:, at] = new_master
        turned[pl.ds(t, 4, 32), :] = new_master
    published[px, pz, pc, py] = turned[...].astype(jnp.bfloat16)

    def spread(stream, axis, fixed, d):
        part = region(published, stream, 0, me, fixed)
        return send(part, part, moved(me, **{axis: d}))

    ready = []
    for stream in (STREAMS[0], STREAMS[1], STREAMS[2]):
        axis = stream[2][2]
        ready.append([spread(stream, axis, {"x": px, "y": py, "z": pz, "c": pc}, d) for d in (2, 1, 3)])
    for level in (1, 0):
        for n, stream in enumerate(STREAMS):
            for copy in ready[n]:
                copy.wait_recv()
            fixed = {"c": pc} | {a: me[a] for a in stream[2][: level + 1]}
            axis = stream[2][level]
            ready[n] = [spread(stream, axis, fixed, d) for d in (2, 1, 3)]
    other = moved(me, c=1)
    passed = []
    for stream in STREAMS:
        part = region(published, stream, 0, me, {"c": pc, stream[2][0]: me[stream[2][0]]})
        passed.append(send(part, part, other))
    for m, d in enumerate((1, 3, 2)):
        for n, stream in enumerate(STREAMS):
            ready[n][(2, 1, 3).index(d)].wait_recv()
            part = region(published, stream, 0, me, {"c": pc, stream[2][0]: (me[stream[2][0]] - d) % 4})
            passed.append(send(part, part, other))
    for copy in passed:
        copy.wait_recv()
    for copy in issued:
        copy.wait_send()


def local(hidden, grad_out, block_list, live_block_count, master, moment, variance):
    i16 = jnp.int16
    state = jax.ShapeDtypeStruct(master.shape, F32)
    vmem, hbm = pl.BlockSpec(memory_space=pltpu.VMEM), pl.BlockSpec(memory_space=pl.ANY)
    first = [pltpu.VMEM((4, 3, 208, 128), i16)] * 4 + [pltpu.VMEM((3, 528, 128), i16)] * 2
    second = [pltpu.VMEM((3, 208, 128), i16)] * 4 + [pltpu.VMEM((3, 144, 128), i16)] * 2
    third = [pltpu.VMEM((3, 64, 128), i16)] * 4 + [pltpu.VMEM((3, 48, 128), i16)] * 2
    copies = 4 + 27 + 18 + 22 + 27 + 12
    *updated, published = pl.pallas_call(
        kernel,
        out_shape=[state] * 4 + [jax.ShapeDtypeStruct((4, 4, 2, 4, 128, 128), jnp.bfloat16)],
        in_specs=[pl.BlockSpec(memory_space=pltpu.SMEM), hbm, hbm, vmem, vmem, vmem, vmem],
        out_specs=[vmem] * 5,
        scratch_shapes=[
            pltpu.VMEM(hidden.shape, jnp.bfloat16),
            pltpu.VMEM(grad_out.shape, jnp.bfloat16),
            pltpu.VMEM(grad_out.shape[::-1], jnp.bfloat16),
            pltpu.VMEM((4, 4, 4, 128, 128), F32),
            pltpu.VMEM((4, 4, 128, 128), F32),
            pltpu.VMEM((4, 2064, 128), i16),
            pltpu.VMEM((4, 2064, 128), i16),
            *first, *second, *third,
            pltpu.VMEM((128, 128), F32),
            pltpu.VMEM((128, 128), F32),
            pltpu.VMEM((2, 8, 128), F32),
            pltpu.VMEM((22, 8, 128), F32),
            pltpu.SemaphoreType.DMA((2,)),
            pltpu.SemaphoreType.DMA((copies,)),
            pltpu.SemaphoreType.DMA((copies,)),
        ],
        compiler_params=pltpu.CompilerParams(
            collective_id=0, has_side_effects=True, vmem_limit_bytes=48 * 2**20
        ),
    )(
        block_list.reshape(-1), hidden, grad_out,
        live_block_count.astype(F32).reshape(1, -1), master, moment, variance,
    )
    return (*updated, published.reshape(master.shape[0] * 128, master.shape[1]))


def solution(mesh):
    one, all_of_it = P(("dp", "owner"), None), P()
    return jax.shard_map(
        local,
        mesh=mesh,
        in_specs=(one, one, all_of_it, all_of_it, one, one, one),
        out_specs=(one, one, one, one, all_of_it),
        check_vma=False,
    )
```

```python
import functools

import jax
import jax.numpy as jnp
from jax import lax
from jax.experimental import pallas as pl
from jax.experimental.pallas import tpu as pltpu
from jax.sharding import PartitionSpec as P

MESH = pl.DeviceIdType.MESH
SIDE = 64
TOKENS = 256
SLAB_ORDER = (2, 1, 3, 0)
STREAMS = ((0, 48, "xyz"), (48, 48, "yzx"), (96, 32, "zxy"))
F32 = jnp.float32


def where_am_i():
    dp = lax.axis_index("dp")
    y = lax.axis_index("owner")
    return {"x": dp // 8, "z": (dp // 2) % 4, "c": dp % 2, "y": y}


def device_at(place):
    return ((place["x"] * 4 + place["z"]) * 2 + place["c"], place["y"])


def moved(me, **by):
    place = dict(me)
    for axis, step in by.items():
        place[axis] = (me[axis] + step) % (2 if axis == "c" else 4)
    return place


def exponent_of(top):
    top = jnp.maximum(jnp.full((16, 128), jnp.max(top), F32), 1e-30)
    return jnp.ceil(jnp.log2(top * (1.0 / 32000.0)))


def encode(values, inverse):
    return jnp.round(values * inverse).astype(jnp.int32).astype(jnp.int16)


def splat(tile):
    return tile[0:1, :].astype(F32)


GATHER = ((0, 384), (1536, 384), (3072, 256))


def region(buf, n, fixed, core=None):
    first, width = GATHER[n]
    start, size = (first + fixed["y"] * width, width) if "y" in fixed else (first, 4 * width)
    index = [fixed.get(a, slice(None)) for a in "xz"] + ([] if core is None else [core])
    return buf.at[(*index, slice(None), pl.ds(start, size))]


def kernel(
    list_hbm, hidden_hbm, grad_out_hbm, live_hbm, master_hbm, moment_hbm, variance_hbm,
    new_master_hbm, new_moment_hbm, new_variance_hbm, clipped_hbm, published,
    list_ref, hidden, grad_out, grad_out_t, live_ref, master_ref, moment_ref, variance_ref,
    new_master_ref, new_moment_ref, new_variance_ref, clipped_ref, acc, pair_part, sib_send, sib_recv,
    send1a, recv1a, send1b, recv1b, send1c, recv1c,
    send2a, recv2a, send2b, recv2b, send2c, recv2c,
    send3a, recv3a, send3b, recv3b, send3c, recv3c,
    turned, flat, sum_send, sum_recv, swap_send, swap_recv, joined, held,
    load_sem, store_sem, send_sem, recv_sem,
):
    me = where_am_i()
    px, py, pz, pc = me["x"], me["y"], me["z"], me["c"]
    loads = [
        pltpu.make_async_copy(grad_out_hbm, grad_out, load_sem.at[0]),
        pltpu.make_async_copy(hidden_hbm, hidden, load_sem.at[1]),
        pltpu.make_async_copy(list_hbm, list_ref, load_sem.at[6]),
        pltpu.make_async_copy(live_hbm, live_ref, load_sem.at[2]),
        pltpu.make_async_copy(master_hbm, master_ref, load_sem.at[3]),
        pltpu.make_async_copy(moment_hbm, moment_ref, load_sem.at[4]),
        pltpu.make_async_copy(variance_hbm, variance_ref, load_sem.at[5]),
    ]
    for load in loads:
        load.start()

    peers = [moved(me, c=1)]
    peers += [moved(me, **{a: d}) for a in "xyz" for d in (1, 2, 3)]
    peers += [moved(me, x=d, c=1) for d in (1, 2, 3)]
    peers += [moved(me, y=i, z=j) for i in (1, 2, 3) for j in (1, 2, 3)]
    barrier = pltpu.get_barrier_semaphore()
    for peer in peers:
        pl.semaphore_signal(barrier, inc=1, device_id=device_at(peer), device_id_type=MESH)

    loads[0].wait()
    for t in range(20):
        grad_out_t[pl.ds(t * 128, 128), :] = grad_out[:, t * 128 : (t + 1) * 128].T
    loads[1].wait()
    loads[2].wait()
    pl.semaphore_wait(barrier, len(peers))

    issued = []

    def send(src, dst, to):
        n = len(issued)
        copy = pltpu.make_async_remote_copy(
            src_ref=src, dst_ref=dst, send_sem=send_sem.at[n], recv_sem=recv_sem.at[n],
            device_id=device_at(to), device_id_type=MESH,
        )
        copy.start()
        issued.append(copy)
        return copy

    lane = lax.broadcasted_iota(jnp.int32, (SIDE, 128), 1)

    low = lane < SIDE

    def two_blocks(pair):
        both, odd = [], []
        for slot in (2 * pair, 2 * pair + 1):
            row, column = list_ref[0, slot], list_ref[1, slot]
            left = grad_out_t[pl.ds(column * SIDE, SIDE), :]
            right = hidden[:, pl.ds((row >> 1) * 128, 128)]
            both.append(jnp.dot(left, right, preferred_element_type=F32))
            odd.append(row & 1)
        crossed = pltpu.roll(jnp.where(low, both[1], both[0]), SIDE, 1)
        straight = jnp.where(low, both[0], both[1])
        return jnp.where(jnp.where(low, odd[0], 1 - odd[1]) == 1, crossed, straight)

    sends1 = []
    for k, step in enumerate(SLAB_ORDER):
        zk = (pz + step) % 4

        def for_sibling(i, top, zk=zk):
            for u in range(16):
                x, y, p = 2 * i + u // 8, (u // 2) % 4, u % 2
                owner = ((x * 4 + zk) * 2 + (1 - pc)) * 4 + y
                part = two_blocks(2 * owner + p)
                pair_part[x, y, pl.ds(p * SIDE, SIDE), :] = part
                top = jnp.maximum(top, jnp.max(jnp.abs(part).reshape(8, 8, 128), axis=0))
            return top

        top = lax.fori_loop(0, 2, for_sibling, jnp.zeros((8, 128), F32))
        exponent = exponent_of(top)
        inverse = jnp.exp2(-exponent)[0:1, :]
        for x in range(4):
            for y in range(4):
                sib_send[k, pl.ds((x * 4 + y) * 128, 128), :] = encode(pair_part[x, y], inverse)
        sib_send[k, pl.ds(2048, 16), :] = exponent.astype(jnp.int32).astype(jnp.int16)
        sib = send(sib_send.at[k], sib_recv.at[k], moved(me, c=1))

        def for_self(i, carry, zk=zk):
            for u in range(16):
                x, y, p = 2 * i + u // 8, (u // 2) % 4, u % 2
                owner = ((x * 4 + zk) * 2 + pc) * 4 + y
                acc[x, zk, y, pl.ds(p * SIDE, SIDE), :] = two_blocks(2 * owner + p)
            return carry

        lax.fori_loop(0, 2, for_self, 0)
        sib.wait_recv()
        scale = jnp.exp2(splat(sib_recv[k, pl.ds(2048, 16), :]))
        top = jnp.zeros((8, 128), F32)
        for x in range(4):
            for y in range(4):
                total = acc[x, zk, y] + scale * sib_recv[k, pl.ds((x * 4 + y) * 128, 128), :].astype(F32)
                acc[x, zk, y] = total
                top = jnp.maximum(top, jnp.max(jnp.abs(total).reshape(16, 8, 128), axis=0))
        exponent = exponent_of(top)
        inverse = jnp.exp2(-exponent)[0:1, :]
        exponent = exponent.astype(jnp.int32).astype(jnp.int16)
        slab = []
        if step:
            for x in range(4):
                for y in range(4):
                    send1c[step - 1, pl.ds((x * 4 + y) * 32, 32), :] = encode(acc[x, zk, y, 96:128, :], inverse)
            send1c[step - 1, pl.ds(512, 16), :] = exponent
            slab.append(send(send1c.at[step - 1], recv1c.at[step - 1], moved(me, z=step)))
        for d in (2, 1, 3):
            to = (px + d) % 4
            for y in range(4):
                send1a[k, d - 1, pl.ds(y * 48, 48), :] = encode(acc[to, zk, y, 0:48, :], inverse)
            send1a[k, d - 1, pl.ds(192, 16), :] = exponent
            slab.append(send(send1a.at[k, d - 1], recv1a.at[k, d - 1], moved(me, x=d)))
            to = (py + d) % 4
            for x in range(4):
                send1b[k, d - 1, pl.ds(x * 48, 48), :] = encode(acc[x, zk, to, 48:96, :], inverse)
            send1b[k, d - 1, pl.ds(192, 16), :] = exponent
            slab.append(send(send1b.at[k, d - 1], recv1b.at[k, d - 1], moved(me, y=d)))
        sends1.append(slab)

    def finish(k):
        step = SLAB_ORDER[k]
        zk = (pz + step) % 4
        slab = list(sends1[k])
        if step:
            slab.pop(0).wait_recv()
            scale = jnp.exp2(splat(recv1c[step - 1, pl.ds(512, 16), :]))
            for x in range(4):
                for y in range(4):
                    acc[x, pz, y, 96:128, :] += scale * recv1c[step - 1, pl.ds((x * 4 + y) * 32, 32), :].astype(F32)
        for n, d in enumerate((2, 1, 3)):
            slab[2 * n].wait_recv()
            scale = jnp.exp2(splat(recv1a[k, d - 1, pl.ds(192, 16), :]))
            for y in range(4):
                acc[px, zk, y, 0:48, :] += scale * recv1a[k, d - 1, pl.ds(y * 48, 48), :].astype(F32)
            slab[2 * n + 1].wait_recv()
            scale = jnp.exp2(splat(recv1b[k, d - 1, pl.ds(192, 16), :]))
            for x in range(4):
                acc[x, zk, py, 48:96, :] += scale * recv1b[k, d - 1, pl.ds(x * 48, 48), :].astype(F32)

    for k in range(4):
        finish(k)

    def later_phase(axis, out_buf, in_buf, rows, first, count, place):
        held = [[acc[(*place(j, (me[axis] + d) % 4), pl.ds(first, rows), slice(None))] for j in range(count)] for d in (2, 1, 3)]
        top = functools.reduce(jnp.maximum, [jnp.max(jnp.abs(v).reshape(rows // 8, 8, 128), axis=0) for h in held for v in h])
        exponent = exponent_of(top)
        inverse = jnp.exp2(-exponent)[0:1, :]
        exponent = exponent.astype(jnp.int32).astype(jnp.int16)
        copies = []
        for h, d in zip(held, (2, 1, 3), strict=True):
            for j, v in enumerate(h):
                out_buf[d - 1, pl.ds(j * rows, rows), :] = encode(v, inverse)
            out_buf[d - 1, pl.ds(count * rows, 16), :] = exponent
            copies.append(send(out_buf.at[d - 1], in_buf.at[d - 1], moved(me, **{axis: d})))

        def add():
            for d, copy in zip((2, 1, 3), copies, strict=True):
                copy.wait_recv()
                scale = jnp.exp2(splat(in_buf[d - 1, pl.ds(count * rows, 16), :]))
                for j in range(count):
                    acc[(*place(j, me[axis]), pl.ds(first, rows), slice(None))] += scale * in_buf[d - 1, pl.ds(j * rows, rows), :].astype(F32)

        return add

    adds = [
        later_phase("x", send2c, recv2c, 32, 96, 4, lambda j, q: (q, pz, j)),
        later_phase("y", send2a, recv2a, 48, 0, 4, lambda j, q: (px, j, q)),
        later_phase("z", send2b, recv2b, 48, 48, 4, lambda j, q: (j, q, py)),
    ]
    adds[0]()
    last = [later_phase("y", send3c, recv3c, 32, 96, 1, lambda j, q: (px, pz, q))]
    adds[1]()
    last.append(later_phase("z", send3a, recv3a, 48, 0, 1, lambda j, q: (px, q, py)))
    adds[2]()
    last.append(later_phase("x", send3b, recv3b, 48, 48, 1, lambda j, q: (q, pz, py)))
    for add in last:
        add()

    for load in loads[3:]:
        load.wait()
    counts = live_ref[0:1, :].astype(F32)
    owner = ((px * 4 + pz) * 2 + pc) * 4 + py
    at = lax.broadcasted_iota(jnp.int32, (1, 128), 1)
    mine = jnp.sum(jnp.where(at == owner, counts, 0.0))
    live_total = jnp.sum(counts) * float(SIDE * SIDE)
    slot = 2 * (lax.broadcasted_iota(jnp.int32, (128, 128), 0) // SIDE) + lax.broadcasted_iota(jnp.int32, (128, 128), 1) // SIDE
    own = jnp.where(slot.astype(F32) < mine, acc[px, pz, py], 0.0)
    sum_send[0] = jnp.full((8, 128), jnp.sum(own * own), F32)
    copies = []
    for n, by in enumerate([{"c": 1}] + [{"x": d, "c": c} for d in (1, 2, 3) for c in (0, 1)]):
        copies.append(send(sum_send.at[0], sum_recv.at[n], moved(me, **by)))
    turned[...] = own.T
    even, odd = turned[pl.ds(0, SIDE, 2), :], turned[pl.ds(1, SIDE, 2), :]
    flat[pl.ds(0, SIDE), :] = jnp.where(lane < SIDE, even, pltpu.roll(odd, SIDE, 1))
    flat[pl.ds(SIDE, SIDE), :] = jnp.where(lane < SIDE, pltpu.roll(even, SIDE, 1), odd)
    square = sum_send[0]
    for n, copy in enumerate(copies):
        copy.wait_recv()
        square += sum_recv[n]
    sum_send[1] = square
    copies = []
    for i in range(4):
        for j in range(4):
            if i or j:
                copies.append(send(sum_send.at[1], sum_recv.at[7 + len(copies)], moved(me, y=i, z=j)))
    for n, copy in enumerate(copies):
        copy.wait_recv()
        square += sum_recv[7 + n]
    mean_square = square[0:4] / live_total
    clip = jnp.minimum(1.0, 1.0 / jnp.sqrt(mean_square + 1e-06))

    for t in range(32):
        at = pl.ds(t * 128, 128)
        clipped = clip * flat[pl.ds(t, 4, 32), :]
        new_moment = 0.9 * moment_ref[:, at] + 0.1 * clipped
        new_variance = 0.95 * variance_ref[:, at] + 0.05 * clipped * clipped
        moment_hat = new_moment / (1.0 - 0.9**20)
        variance_hat = new_variance / (1.0 - 0.95**20)
        master = master_ref[:, at]
        new_master = master - 0.02 * (moment_hat / (jnp.sqrt(variance_hat) + 1e-08) + 0.1 * master)
        clipped_ref[:, at] = clipped
        new_moment_ref[:, at] = new_moment
        new_variance_ref[:, at] = new_variance
        new_master_ref[:, at] = new_master
        to, part = divmod(t, 3) if t < 12 else divmod(t - 12, 3) if t < 24 else divmod(t - 24, 2)
        part += 0 if t < 12 else 3 if t < 24 else 6
        swap_send[to, part // 2, pl.ds(4 * (part % 2), 4), :] = new_master
    copies = [send(swap_send.at[(py + d) % 4], swap_recv.at[py], moved(me, y=d)) for d in (2, 1, 3)]
    stores = []

    def store(src, dst):
        copy = pltpu.make_async_copy(src, dst, store_sem.at[len(stores)])
        copy.start()
        stores.append(copy)

    store(new_master_ref, new_master_hbm)
    store(new_moment_ref, new_moment_hbm)
    store(new_variance_ref, new_variance_hbm)
    store(clipped_ref, clipped_hbm)
    swap_recv[py] = swap_send[py]
    for copy in copies:
        copy.wait_recv()
    for part in range(8):
        for source in range(4):
            joined[part, pl.ds(4 * source, 4), :] = swap_recv[source, part // 2, pl.ds(4 * (part % 2), 4), :]
    part = 0
    for first, width in GATHER:
        for column in range(0, width, 128):
            at = pl.multiple_of(first + column + py * width, 128)
            held[px, pz, :, pl.ds(at, 128)] = joined[part].astype(jnp.bfloat16)
            part += 1

    def spread(n, fixed, axis):
        part = region(held, n, fixed)
        return {d: send(part, part, moved(me, **{axis: d})) for d in (2, 1, 3)}

    orders = [order for _, _, order in STREAMS]
    inner = [spread(n, {"x": px, "y": py, "z": pz}, order[2]) for n, order in enumerate(orders)]
    middle, outer = [], []
    for n, order in enumerate(orders):
        for copy in inner[n].values():
            copy.wait_recv()
        middle.append(spread(n, {a: me[a] for a in order[:2]}, order[1]))
    for n, order in enumerate(orders):
        outer.append([spread(n, {a: me[a] for a in order[:2]}, order[0])])
    for d in (1, 3, 2):
        for n, order in enumerate(orders):
            middle[n][d].wait_recv()
            outer[n].append(spread(n, {order[0]: me[order[0]], order[1]: (me[order[1]] - d) % 4}, order[0]))
    other = moved(me, c=1)
    passed = []

    def settle(n, fixed):
        part, place = region(held, n, fixed), region(published, n, fixed, pc)
        passed.append(send(part, place, other))
        store(part, place)

    for n, order in enumerate(orders):
        settle(n, {order[0]: me[order[0]]})
    for d in (1, 3, 2):
        for n, order in enumerate(orders):
            for piece in outer[n]:
                piece[d].wait_recv()
            settle(n, {order[0]: (me[order[0]] - d) % 4})
    for copy in passed:
        copy.wait_recv()
    for copy in issued:
        copy.wait_send()
    for copy in stores:
        copy.wait()


def local(hidden, grad_out, block_list, live_block_count, master, moment, variance):
    i16 = jnp.int16
    state = jax.ShapeDtypeStruct(master.shape, F32)
    vmem, hbm = pl.BlockSpec(memory_space=pltpu.VMEM), pl.BlockSpec(memory_space=pltpu.HBM)
    first = [pltpu.VMEM((4, 3, 208, 128), i16)] * 4 + [pltpu.VMEM((3, 528, 128), i16)] * 2
    second = [pltpu.VMEM((3, 208, 128), i16)] * 4 + [pltpu.VMEM((3, 144, 128), i16)] * 2
    third = [pltpu.VMEM((3, 64, 128), i16)] * 4 + [pltpu.VMEM((3, 48, 128), i16)] * 2
    copies = 4 + 27 + 18 + 22 + 3 + 9 + 9 + 36 + 12
    *updated, published = pl.pallas_call(
        kernel,
        out_shape=[state] * 4 + [jax.ShapeDtypeStruct((4, 4, 2, 16, 4096), jnp.bfloat16)],
        in_specs=[hbm] * 7,
        out_specs=[hbm] * 5,
        scratch_shapes=[
            pltpu.SMEM(block_list.shape[::-1], jnp.int32),
            pltpu.VMEM(hidden.shape, jnp.bfloat16),
            pltpu.VMEM(grad_out.shape, jnp.bfloat16),
            pltpu.VMEM(grad_out.shape[::-1], jnp.bfloat16),
            pltpu.VMEM((1, live_block_count.shape[0]), jnp.int32),
            *[pltpu.VMEM(master.shape, F32)] * 7,
            pltpu.VMEM((4, 4, 4, 128, 128), F32),
            pltpu.VMEM((4, 4, 128, 128), F32),
            pltpu.VMEM((4, 2064, 128), i16),
            pltpu.VMEM((4, 2064, 128), i16),
            *first, *second, *third,
            pltpu.VMEM((128, 128), F32),
            pltpu.VMEM((128, 128), F32),
            pltpu.VMEM((2, 8, 128), F32),
            pltpu.VMEM((22, 8, 128), F32),
            pltpu.VMEM((4, 4, 8, 128), F32),
            pltpu.VMEM((4, 4, 8, 128), F32),
            pltpu.VMEM((8, 16, 128), F32),
            pltpu.VMEM((4, 4, 16, 4096), jnp.bfloat16),
            pltpu.SemaphoreType.DMA((7,)),
            pltpu.SemaphoreType.DMA((16,)),
            pltpu.SemaphoreType.DMA((copies,)),
            pltpu.SemaphoreType.DMA((copies,)),
        ],
        compiler_params=pltpu.CompilerParams(
            collective_id=0, has_side_effects=True, vmem_limit_bytes=30 * 2**20
        ),
    )(
        *[pltpu.with_memory_space_constraint(a, pltpu.HBM) for a in (block_list.T, hidden, grad_out, live_block_count.reshape(1, -1), master, moment, variance)],
    )
    return (*updated, published.reshape(512, 4096))


def solution(mesh):
    one, all_of_it = P(("dp", "owner"), None), P()
    return jax.shard_map(
        local,
        mesh=mesh,
        in_specs=(one, one, all_of_it, all_of_it, one, one, one),
        out_specs=(one, one, one, one, all_of_it),
        check_vma=False,
    )
```

```python
import functools

import jax
import jax.numpy as jnp
from jax import lax
from jax.experimental import pallas as pl
from jax.experimental.pallas import tpu as pltpu
from jax.sharding import PartitionSpec as P

MESH = pl.DeviceIdType.MESH
SIDE = 64
TOKENS = 256
SLAB_ORDER = (2, 1, 3, 0)
STREAMS = ((0, 48, "xyz"), (48, 48, "yzx"), (96, 32, "zxy"))
F32 = jnp.float32


def where_am_i():
    dp = lax.axis_index("dp")
    y = lax.axis_index("owner")
    return {"x": dp // 8, "z": (dp // 2) % 4, "c": dp % 2, "y": y}


def device_at(place):
    return ((place["x"] * 4 + place["z"]) * 2 + place["c"], place["y"])


def moved(me, **by):
    place = dict(me)
    for axis, step in by.items():
        place[axis] = (me[axis] + step) % (2 if axis == "c" else 4)
    return place


def exponent_of(top):
    top = jnp.maximum(jnp.full((16, 128), jnp.max(top), F32), 1e-30)
    return jnp.ceil(jnp.log2(top * (1.0 / 32000.0)))


def encode(values, inverse):
    return jnp.round(values * inverse).astype(jnp.int32).astype(jnp.int16)


def splat(tile):
    return tile[0:1, :].astype(F32)


GATHER = ((0, 384), (1536, 384), (3072, 256))


def region(buf, n, fixed, core=None):
    first, width = GATHER[n]
    start, size = (first + fixed["y"] * width, width) if "y" in fixed else (first, 4 * width)
    index = [fixed.get(a, slice(None)) for a in "xz"] + ([] if core is None else [core])
    return buf.at[(*index, slice(None), pl.ds(start, size))]


def part_of(t):
    to, part = divmod(t, 3) if t < 12 else divmod(t - 12, 3) if t < 24 else divmod(t - 24, 2)
    return to, part + (0 if t < 12 else 3 if t < 24 else 6)


def adamw(clipped, master, moment, variance):
    new_moment = 0.9 * moment + 0.1 * clipped
    new_variance = 0.95 * variance + 0.05 * clipped * clipped
    moment_hat = new_moment / (1.0 - 0.9**20)
    variance_hat = new_variance / (1.0 - 0.95**20)
    new_master = master - 0.02 * (moment_hat / (jnp.sqrt(variance_hat) + 1e-08) + 0.1 * master)
    return new_master, new_moment, new_variance


def kernel(
    list_hbm, hidden_hbm, grad_out_hbm, live_hbm, master_hbm, moment_hbm, variance_hbm,
    new_master_hbm, new_moment_hbm, new_variance_hbm, clipped_hbm, published,
    list_ref, hidden, grad_out, grad_out_t, live_ref, master_ref, moment_ref, variance_ref,
    new_master_ref, new_moment_ref, new_variance_ref, clipped_ref, acc, pair_part, sib_send, sib_recv,
    send1a, recv1a, send1b, recv1b, send1c, recv1c,
    send2a, recv2a, send2b, recv2b, send2c, recv2c,
    send3a, recv3a, send3b, recv3b, send3c, recv3c,
    turned, flat, sum_send, sum_recv, swap_send, swap_recv, state_send, state_recv, joined, held,
    load_sem, store_sem, send_sem, recv_sem,
):
    me = where_am_i()
    px, py, pz, pc = me["x"], me["y"], me["z"], me["c"]
    loads = [
        pltpu.make_async_copy(grad_out_hbm, grad_out, load_sem.at[0]),
        pltpu.make_async_copy(hidden_hbm, hidden, load_sem.at[1]),
        pltpu.make_async_copy(list_hbm, list_ref, load_sem.at[6]),
        pltpu.make_async_copy(live_hbm, live_ref, load_sem.at[2]),
        pltpu.make_async_copy(master_hbm, master_ref, load_sem.at[3]),
        pltpu.make_async_copy(moment_hbm, moment_ref, load_sem.at[4]),
        pltpu.make_async_copy(variance_hbm, variance_ref, load_sem.at[5]),
    ]
    for load in loads:
        load.start()

    peers = [moved(me, c=1)]
    peers += [moved(me, **{a: d}) for a in "xyz" for d in (1, 2, 3)]
    peers += [moved(me, x=d, c=1) for d in (1, 2, 3)]
    peers += [moved(me, y=i, z=j) for i in (1, 2, 3) for j in (1, 2, 3)]
    barrier = pltpu.get_barrier_semaphore()
    for peer in peers:
        pl.semaphore_signal(barrier, inc=1, device_id=device_at(peer), device_id_type=MESH)

    loads[0].wait()
    for t in range(20):
        grad_out_t[pl.ds(t * 128, 128), :] = grad_out[:, t * 128 : (t + 1) * 128].T
    for load in loads[3:]:
        load.wait()
    for n, ref in enumerate((master_ref, moment_ref, variance_ref)):
        for t in range(32):
            to, part = part_of(t)
            state_send[to, n, part // 2, pl.ds(4 * (part % 2), 4), :] = ref[:, t * 128 : (t + 1) * 128]
    state_recv[py] = state_send[py]
    loads[1].wait()
    loads[2].wait()
    pl.semaphore_wait(barrier, len(peers))

    issued = []

    def send(src, dst, to):
        n = len(issued)
        copy = pltpu.make_async_remote_copy(
            src_ref=src, dst_ref=dst, send_sem=send_sem.at[n], recv_sem=recv_sem.at[n],
            device_id=device_at(to), device_id_type=MESH,
        )
        copy.start()
        issued.append(copy)
        return copy

    state_copies = [send(state_send.at[(py + d) % 4], state_recv.at[py], moved(me, y=d)) for d in (2, 1, 3)]
    lane = lax.broadcasted_iota(jnp.int32, (SIDE, 128), 1)

    low = lane < SIDE

    def two_blocks(pair):
        both, odd = [], []
        for slot in (2 * pair, 2 * pair + 1):
            row, column = list_ref[0, slot], list_ref[1, slot]
            left = grad_out_t[pl.ds(column * SIDE, SIDE), :]
            right = hidden[:, pl.ds((row >> 1) * 128, 128)]
            both.append(jnp.dot(left, right, preferred_element_type=F32))
            odd.append(row & 1)
        crossed = pltpu.roll(jnp.where(low, both[1], both[0]), SIDE, 1)
        straight = jnp.where(low, both[0], both[1])
        return jnp.where(jnp.where(low, odd[0], 1 - odd[1]) == 1, crossed, straight)

    sends1 = []
    for k, step in enumerate(SLAB_ORDER):
        zk = (pz + step) % 4

        def for_sibling(i, top, zk=zk):
            for u in range(16):
                x, y, p = 2 * i + u // 8, (u // 2) % 4, u % 2
                owner = ((x * 4 + zk) * 2 + (1 - pc)) * 4 + y
                part = two_blocks(2 * owner + p)
                pair_part[x, y, pl.ds(p * SIDE, SIDE), :] = part
                top = jnp.maximum(top, jnp.max(jnp.abs(part).reshape(8, 8, 128), axis=0))
            return top

        top = lax.fori_loop(0, 2, for_sibling, jnp.zeros((8, 128), F32))
        exponent = exponent_of(top)
        inverse = jnp.exp2(-exponent)[0:1, :]
        for x in range(4):
            for y in range(4):
                sib_send[k, pl.ds((x * 4 + y) * 128, 128), :] = encode(pair_part[x, y], inverse)
        sib_send[k, pl.ds(2048, 16), :] = exponent.astype(jnp.int32).astype(jnp.int16)
        sib = send(sib_send.at[k], sib_recv.at[k], moved(me, c=1))

        def for_self(i, carry, zk=zk):
            for u in range(16):
                x, y, p = 2 * i + u // 8, (u // 2) % 4, u % 2
                owner = ((x * 4 + zk) * 2 + pc) * 4 + y
                acc[x, zk, y, pl.ds(p * SIDE, SIDE), :] = two_blocks(2 * owner + p)
            return carry

        lax.fori_loop(0, 2, for_self, 0)
        sib.wait_recv()
        scale = jnp.exp2(splat(sib_recv[k, pl.ds(2048, 16), :]))
        top = jnp.zeros((8, 128), F32)
        for x in range(4):
            for y in range(4):
                total = acc[x, zk, y] + scale * sib_recv[k, pl.ds((x * 4 + y) * 128, 128), :].astype(F32)
                acc[x, zk, y] = total
                top = jnp.maximum(top, jnp.max(jnp.abs(total).reshape(16, 8, 128), axis=0))
        exponent = exponent_of(top)
        inverse = jnp.exp2(-exponent)[0:1, :]
        exponent = exponent.astype(jnp.int32).astype(jnp.int16)
        slab = []
        if step:
            for x in range(4):
                for y in range(4):
                    send1c[step - 1, pl.ds((x * 4 + y) * 32, 32), :] = encode(acc[x, zk, y, 96:128, :], inverse)
            send1c[step - 1, pl.ds(512, 16), :] = exponent
            slab.append(send(send1c.at[step - 1], recv1c.at[step - 1], moved(me, z=step)))
        for d in (2, 1, 3):
            to = (px + d) % 4
            for y in range(4):
                send1a[k, d - 1, pl.ds(y * 48, 48), :] = encode(acc[to, zk, y, 0:48, :], inverse)
            send1a[k, d - 1, pl.ds(192, 16), :] = exponent
            slab.append(send(send1a.at[k, d - 1], recv1a.at[k, d - 1], moved(me, x=d)))
            to = (py + d) % 4
            for x in range(4):
                send1b[k, d - 1, pl.ds(x * 48, 48), :] = encode(acc[x, zk, to, 48:96, :], inverse)
            send1b[k, d - 1, pl.ds(192, 16), :] = exponent
            slab.append(send(send1b.at[k, d - 1], recv1b.at[k, d - 1], moved(me, y=d)))
        sends1.append(slab)

    def finish(k):
        step = SLAB_ORDER[k]
        zk = (pz + step) % 4
        slab = list(sends1[k])
        if step:
            slab.pop(0).wait_recv()
            scale = jnp.exp2(splat(recv1c[step - 1, pl.ds(512, 16), :]))
            for x in range(4):
                for y in range(4):
                    acc[x, pz, y, 96:128, :] += scale * recv1c[step - 1, pl.ds((x * 4 + y) * 32, 32), :].astype(F32)
        for n, d in enumerate((2, 1, 3)):
            slab[2 * n].wait_recv()
            scale = jnp.exp2(splat(recv1a[k, d - 1, pl.ds(192, 16), :]))
            for y in range(4):
                acc[px, zk, y, 0:48, :] += scale * recv1a[k, d - 1, pl.ds(y * 48, 48), :].astype(F32)
            slab[2 * n + 1].wait_recv()
            scale = jnp.exp2(splat(recv1b[k, d - 1, pl.ds(192, 16), :]))
            for x in range(4):
                acc[x, zk, py, 48:96, :] += scale * recv1b[k, d - 1, pl.ds(x * 48, 48), :].astype(F32)

    for k in range(4):
        finish(k)

    def later_phase(axis, out_buf, in_buf, rows, first, count, place):
        held = [[acc[(*place(j, (me[axis] + d) % 4), pl.ds(first, rows), slice(None))] for j in range(count)] for d in (2, 1, 3)]
        top = functools.reduce(jnp.maximum, [jnp.max(jnp.abs(v).reshape(rows // 8, 8, 128), axis=0) for h in held for v in h])
        exponent = exponent_of(top)
        inverse = jnp.exp2(-exponent)[0:1, :]
        exponent = exponent.astype(jnp.int32).astype(jnp.int16)
        copies = []
        for h, d in zip(held, (2, 1, 3), strict=True):
            for j, v in enumerate(h):
                out_buf[d - 1, pl.ds(j * rows, rows), :] = encode(v, inverse)
            out_buf[d - 1, pl.ds(count * rows, 16), :] = exponent
            copies.append(send(out_buf.at[d - 1], in_buf.at[d - 1], moved(me, **{axis: d})))

        def add():
            for d, copy in zip((2, 1, 3), copies, strict=True):
                copy.wait_recv()
                scale = jnp.exp2(splat(in_buf[d - 1, pl.ds(count * rows, 16), :]))
                for j in range(count):
                    acc[(*place(j, me[axis]), pl.ds(first, rows), slice(None))] += scale * in_buf[d - 1, pl.ds(j * rows, rows), :].astype(F32)

        return add

    adds = [
        later_phase("x", send2c, recv2c, 32, 96, 4, lambda j, q: (q, pz, j)),
        later_phase("y", send2a, recv2a, 48, 0, 4, lambda j, q: (px, j, q)),
        later_phase("z", send2b, recv2b, 48, 48, 4, lambda j, q: (j, q, py)),
    ]
    adds[0]()
    last = [later_phase("y", send3c, recv3c, 32, 96, 1, lambda j, q: (px, pz, q))]
    adds[1]()
    last.append(later_phase("z", send3a, recv3a, 48, 0, 1, lambda j, q: (px, q, py)))
    adds[2]()
    last.append(later_phase("x", send3b, recv3b, 48, 48, 1, lambda j, q: (q, pz, py)))
    for add in last:
        add()

    counts = live_ref[0:1, :].astype(F32)
    owner = ((px * 4 + pz) * 2 + pc) * 4 + py
    at = lax.broadcasted_iota(jnp.int32, (1, 128), 1)
    mine = jnp.sum(jnp.where(at == owner, counts, 0.0))
    live_total = jnp.sum(counts) * float(SIDE * SIDE)
    slot = 2 * (lax.broadcasted_iota(jnp.int32, (128, 128), 0) // SIDE) + lax.broadcasted_iota(jnp.int32, (128, 128), 1) // SIDE
    own = jnp.where(slot.astype(F32) < mine, acc[px, pz, py], 0.0)
    sum_send[0] = jnp.full((8, 128), jnp.sum(own * own), F32)
    copies = []
    for n, by in enumerate([{"c": 1}] + [{"x": d, "c": c} for d in (1, 2, 3) for c in (0, 1)]):
        copies.append(send(sum_send.at[0], sum_recv.at[n], moved(me, **by)))
    turned[...] = own.T
    even, odd = turned[pl.ds(0, SIDE, 2), :], turned[pl.ds(1, SIDE, 2), :]
    flat[pl.ds(0, SIDE), :] = jnp.where(lane < SIDE, even, pltpu.roll(odd, SIDE, 1))
    flat[pl.ds(SIDE, SIDE), :] = jnp.where(lane < SIDE, pltpu.roll(even, SIDE, 1), odd)
    for t in range(32):
        to, part = part_of(t)
        swap_send[to, part // 2, pl.ds(4 * (part % 2), 4), :] = flat[pl.ds(t, 4, 32), :]
    swaps = [send(swap_send.at[(py + d) % 4], swap_recv.at[py], moved(me, y=d)) for d in (2, 1, 3)]
    swap_recv[py] = swap_send[py]
    square = sum_send[0]
    for n, copy in enumerate(copies):
        copy.wait_recv()
        square += sum_recv[n]
    sum_send[1] = square
    copies = []
    for i in range(4):
        for j in range(4):
            if i or j:
                copies.append(send(sum_send.at[1], sum_recv.at[7 + len(copies)], moved(me, y=i, z=j)))
    for n, copy in enumerate(copies):
        copy.wait_recv()
        square += sum_recv[7 + n]
    for copy in swaps + state_copies:
        copy.wait_recv()
    mean_square = square / live_total
    clip = jnp.minimum(1.0, 1.0 / jnp.sqrt(mean_square + 1e-06))

    for part in range(8):
        for source in range(4):
            rows, at = pl.ds(4 * source, 4), pl.ds(4 * (part % 2), 4)
            joined[3, part, rows, :] = swap_recv[source, part // 2, at, :]
            for n in range(3):
                joined[n, part, rows, :] = state_recv[source, n, part // 2, at, :]
    part = 0
    for first, width in GATHER:
        for column in range(0, width, 128):
            at = pl.multiple_of(first + column + py * width, 128)
            new_master, _, _ = adamw(clip[0:1] * joined[3, part], joined[0, part], joined[1, part], joined[2, part])
            held[px, pz, :, pl.ds(at, 128)] = new_master.astype(jnp.bfloat16)
            part += 1

    def spread(n, fixed, axis):
        part = region(held, n, fixed)
        return {d: send(part, part, moved(me, **{axis: d})) for d in (2, 1, 3)}

    orders = [order for _, _, order in STREAMS]
    inner = [spread(n, {"x": px, "y": py, "z": pz}, order[2]) for n, order in enumerate(orders)]
    for t in range(32):
        at = pl.ds(t * 128, 128)
        clipped = clip[0:4] * flat[pl.ds(t, 4, 32), :]
        new_master, new_moment, new_variance = adamw(clipped, master_ref[:, at], moment_ref[:, at], variance_ref[:, at])
        clipped_ref[:, at] = clipped
        new_moment_ref[:, at] = new_moment
        new_variance_ref[:, at] = new_variance
        new_master_ref[:, at] = new_master
    stores = []

    def store(src, dst):
        copy = pltpu.make_async_copy(src, dst, store_sem.at[len(stores)])
        copy.start()
        stores.append(copy)

    store(new_master_ref, new_master_hbm)
    store(new_moment_ref, new_moment_hbm)
    store(new_variance_ref, new_variance_hbm)
    store(clipped_ref, clipped_hbm)
    middle, outer = [], []
    for n, order in enumerate(orders):
        for copy in inner[n].values():
            copy.wait_recv()
        middle.append(spread(n, {a: me[a] for a in order[:2]}, order[1]))
    for n, order in enumerate(orders):
        outer.append([spread(n, {a: me[a] for a in order[:2]}, order[0])])
    for d in (1, 3, 2):
        for n, order in enumerate(orders):
            middle[n][d].wait_recv()
            outer[n].append(spread(n, {order[0]: me[order[0]], order[1]: (me[order[1]] - d) % 4}, order[0]))
    other = moved(me, c=1)
    passed = []

    def settle(n, fixed):
        part, place = region(held, n, fixed), region(published, n, fixed, pc)
        passed.append(send(part, place, other))
        store(part, place)

    for n, order in enumerate(orders):
        settle(n, {order[0]: me[order[0]]})
    for d in (1, 3, 2):
        for n, order in enumerate(orders):
            for piece in outer[n]:
                piece[d].wait_recv()
            settle(n, {order[0]: (me[order[0]] - d) % 4})
    for copy in passed:
        copy.wait_recv()
    for copy in issued:
        copy.wait_send()
    for copy in stores:
        copy.wait()


def pass_on(*refs):
    sources, results, sem = refs[:5], refs[5:10], refs[10]
    copies = []
    for i in range(4):
        rows = pl.ds(i * 128, 128)
        copies.append(pltpu.make_async_copy(sources[4].at[rows], results[4].at[rows], sem.at[i]))
        copies.append(pltpu.make_async_copy(sources[i], results[i], sem.at[4 + i]))
    for copy in copies:
        copy.start()
    for copy in copies:
        copy.wait()


def local(hidden, grad_out, block_list, live_block_count, master, moment, variance):
    i16 = jnp.int16
    state = jax.ShapeDtypeStruct(master.shape, F32)
    vmem, hbm = pl.BlockSpec(memory_space=pltpu.VMEM), pl.BlockSpec(memory_space=pltpu.HBM)
    first = [pltpu.VMEM((4, 3, 208, 128), i16)] * 4 + [pltpu.VMEM((3, 528, 128), i16)] * 2
    second = [pltpu.VMEM((3, 208, 128), i16)] * 4 + [pltpu.VMEM((3, 144, 128), i16)] * 2
    third = [pltpu.VMEM((3, 64, 128), i16)] * 4 + [pltpu.VMEM((3, 48, 128), i16)] * 2
    copies = 4 + 27 + 18 + 22 + 3 + 3 + 9 + 9 + 36 + 12
    *updated, published = pl.pallas_call(
        kernel,
        out_shape=[state] * 4 + [jax.ShapeDtypeStruct((4, 4, 2, 16, 4096), jnp.bfloat16)],
        in_specs=[hbm] * 7,
        out_specs=[hbm] * 5,
        scratch_shapes=[
            pltpu.SMEM(block_list.shape[::-1], jnp.int32),
            pltpu.VMEM(hidden.shape, jnp.bfloat16),
            pltpu.VMEM(grad_out.shape, jnp.bfloat16),
            pltpu.VMEM(grad_out.shape[::-1], jnp.bfloat16),
            pltpu.VMEM((1, live_block_count.shape[0]), jnp.int32),
            *[pltpu.VMEM(master.shape, F32)] * 7,
            pltpu.VMEM((4, 4, 4, 128, 128), F32),
            pltpu.VMEM((4, 4, 128, 128), F32),
            pltpu.VMEM((4, 2064, 128), i16),
            pltpu.VMEM((4, 2064, 128), i16),
            *first, *second, *third,
            pltpu.VMEM((128, 128), F32),
            pltpu.VMEM((128, 128), F32),
            pltpu.VMEM((2, 8, 128), F32),
            pltpu.VMEM((22, 8, 128), F32),
            pltpu.VMEM((4, 4, 8, 128), F32),
            pltpu.VMEM((4, 4, 8, 128), F32),
            pltpu.VMEM((4, 3, 4, 8, 128), F32),
            pltpu.VMEM((4, 3, 4, 8, 128), F32),
            pltpu.VMEM((4, 8, 16, 128), F32),
            pltpu.VMEM((4, 4, 16, 4096), jnp.bfloat16),
            pltpu.SemaphoreType.DMA((7,)),
            pltpu.SemaphoreType.DMA((16,)),
            pltpu.SemaphoreType.DMA((copies,)),
            pltpu.SemaphoreType.DMA((copies,)),
        ],
        compiler_params=pltpu.CompilerParams(
            collective_id=0, has_side_effects=True, vmem_limit_bytes=30 * 2**20
        ),
    )(
        *[pltpu.with_memory_space_constraint(a, pltpu.HBM) for a in (block_list.T, hidden, grad_out, live_block_count.reshape(1, -1), master, moment, variance)],
    )
    return pl.pallas_call(
        pass_on,
        out_shape=[state] * 4 + [jax.ShapeDtypeStruct((512, 4096), jnp.bfloat16)],
        in_specs=[hbm] * 5,
        out_specs=[hbm] * 5,
        scratch_shapes=[pltpu.SemaphoreType.DMA((8,))],
        compiler_params=pltpu.CompilerParams(vmem_limit_bytes=2**20),
    )(*updated, published.reshape(512, 4096))


def solution(mesh):
    one, all_of_it = P(("dp", "owner"), None), P()
    return jax.shard_map(
        local,
        mesh=mesh,
        in_specs=(one, one, all_of_it, all_of_it, one, one, one),
        out_specs=(one, one, one, one, all_of_it),
        check_vma=False,
    )
```

```python
import functools

import jax
import jax.numpy as jnp
from jax import lax
from jax.experimental import pallas as pl
from jax.experimental.pallas import tpu as pltpu
from jax.sharding import PartitionSpec as P

MESH = pl.DeviceIdType.MESH
SIDE = 64
UNROLL = 32
SLAB_ORDER = (2, 1, 3, 0)
STREAMS = ((0, 48, "xyz"), (48, 48, "yzx"), (96, 32, "zxy"))
F32 = jnp.float32


def where_am_i():
    dp = lax.axis_index("dp")
    y = lax.axis_index("owner")
    return {"x": dp // 8, "z": (dp // 2) % 4, "c": dp % 2, "y": y}


def device_at(place):
    return ((place["x"] * 4 + place["z"]) * 2 + place["c"], place["y"])


def moved(me, **by):
    place = dict(me)
    for axis, step in by.items():
        place[axis] = (me[axis] + step) % (2 if axis == "c" else 4)
    return place


def exponent_of(top):
    top = jnp.maximum(jnp.full((16, 128), jnp.max(top), F32), 1e-30)
    return jnp.ceil(jnp.log2(top * (1.0 / 32000.0)))


def encode(values, inverse):
    return jnp.round(values * inverse).astype(jnp.int32).astype(jnp.int16)


def splat(tile):
    return tile[0:1, :].astype(F32)


GATHER = ((0, 384), (1536, 384), (3072, 256))


def region(buf, n, fixed, core=None):
    first, width = GATHER[n]
    start, size = (first + fixed["y"] * width, width) if "y" in fixed else (first, 4 * width)
    index = [fixed.get(a, slice(None)) for a in "xz"] + ([] if core is None else [core])
    return buf.at[(*index, slice(None), pl.ds(start, size))]


def part_of(t):
    to, part = divmod(t, 3) if t < 12 else divmod(t - 12, 3) if t < 24 else divmod(t - 24, 2)
    return to, part + (0 if t < 12 else 3 if t < 24 else 6)


def adamw(clipped, master, moment, variance):
    new_moment = 0.9 * moment + 0.1 * clipped
    new_variance = 0.95 * variance + 0.05 * clipped * clipped
    moment_hat = new_moment / (1.0 - 0.9**20)
    variance_hat = new_variance / (1.0 - 0.95**20)
    new_master = master - 0.02 * (moment_hat / (jnp.sqrt(variance_hat) + 1e-08) + 0.1 * master)
    return new_master, new_moment, new_variance


def kernel(
    list_hbm, hidden_hbm, grad_out_hbm, live_hbm, master_hbm, moment_hbm, variance_hbm,
    new_master_hbm, new_moment_hbm, new_variance_hbm, clipped_hbm, published,
    list_ref, hidden, grad_out, grad_out_t, live_ref, master_ref, moment_ref, variance_ref,
    new_master_ref, new_moment_ref, new_variance_ref, clipped_ref, acc, pair_part, sib_send, sib_recv,
    send1a, recv1a, send1b, recv1b, send1c, recv1c,
    send2a, recv2a, send2b, recv2b, send2c, recv2c,
    send3a, recv3a, send3b, recv3b, send3c, recv3c,
    turned, flat, sum_send, sum_recv, swap_send, swap_recv, state_send, state_recv, joined, held,
    load_sem, store_sem, send_sem, recv_sem,
):
    me = where_am_i()
    px, py, pz, pc = me["x"], me["y"], me["z"], me["c"]
    peers = [moved(me, c=1)]
    peers += [moved(me, **{a: d}) for a in "xyz" for d in (1, 2, 3)]
    peers += [moved(me, x=d, c=1) for d in (1, 2, 3)]
    peers += [moved(me, y=i, z=j) for i in (1, 2, 3) for j in (1, 2, 3)]
    barrier = pltpu.get_barrier_semaphore()
    for peer in peers:
        pl.semaphore_signal(barrier, inc=1, device_id=device_at(peer), device_id_type=MESH)

    loads = [
        pltpu.make_async_copy(grad_out_hbm, grad_out, load_sem.at[0]),
        pltpu.make_async_copy(hidden_hbm, hidden, load_sem.at[1]),
        pltpu.make_async_copy(list_hbm, list_ref, load_sem.at[6]),
        pltpu.make_async_copy(live_hbm, live_ref, load_sem.at[2]),
        pltpu.make_async_copy(master_hbm, master_ref, load_sem.at[3]),
        pltpu.make_async_copy(moment_hbm, moment_ref, load_sem.at[4]),
        pltpu.make_async_copy(variance_hbm, variance_ref, load_sem.at[5]),
    ]
    for load in loads:
        load.start()

    loads[0].wait()
    for t in range(20):
        grad_out_t[pl.ds(t * 128, 128), :] = grad_out[:, t * 128 : (t + 1) * 128].T
    loads[1].wait()
    loads[2].wait()
    pl.semaphore_wait(barrier, len(peers))

    issued = []

    def send(src, dst, to):
        n = len(issued)
        copy = pltpu.make_async_remote_copy(
            src_ref=src, dst_ref=dst, send_sem=send_sem.at[n], recv_sem=recv_sem.at[n],
            device_id=device_at(to), device_id_type=MESH,
        )
        copy.start()
        issued.append(copy)
        return copy

    lane = lax.broadcasted_iota(jnp.int32, (SIDE, 128), 1)

    low = lane < SIDE

    def two_blocks(pair):
        both, odd = [], []
        for slot in (2 * pair, 2 * pair + 1):
            row, column = list_ref[0, slot], list_ref[1, slot]
            left = grad_out_t[pl.ds(column * SIDE, SIDE), :]
            right = hidden[:, pl.ds((row >> 1) * 128, 128)]
            both.append(jnp.dot(left, right, preferred_element_type=F32))
            odd.append(row & 1)
        crossed = pltpu.roll(jnp.where(low, both[1], both[0]), SIDE, 1)
        straight = jnp.where(low, both[0], both[1])
        return jnp.where(jnp.where(low, odd[0], 1 - odd[1]) == 1, crossed, straight)

    def swap_state():
        for load in loads[3:]:
            load.wait()
        for n, ref in enumerate((master_ref, moment_ref, variance_ref)):
            for t in range(32):
                to, part = part_of(t)
                state_send[to, n, part // 2, pl.ds(4 * (part % 2), 4), :] = ref[:, t * 128 : (t + 1) * 128]
        state_recv[py] = state_send[py]
        return [send(state_send.at[(py + d) % 4], state_recv.at[py], moved(me, y=d)) for d in (2, 1, 3)]

    sends1, to_sibling = [], []

    def first_half(k):
        zk = (pz + SLAB_ORDER[k]) % 4

        def for_sibling(i, top):
            for u in range(UNROLL):
                n = UNROLL * i + u
                x, y, p = n // 8, (n // 2) % 4, n % 2
                owner = ((x * 4 + zk) * 2 + (1 - pc)) * 4 + y
                part = two_blocks(2 * owner + p)
                pair_part[x, y, pl.ds(p * SIDE, SIDE), :] = part
                top = jnp.maximum(top, jnp.max(jnp.abs(part).reshape(8, 8, 128), axis=0))
            return top

        top = lax.fori_loop(0, 32 // UNROLL, for_sibling, jnp.zeros((8, 128), F32))
        exponent = exponent_of(top)
        inverse = jnp.exp2(-exponent)[0:1, :]
        for x in range(4):
            for y in range(4):
                sib_send[k, pl.ds((x * 4 + y) * 128, 128), :] = encode(pair_part[x, y], inverse)
        sib_send[k, pl.ds(2048, 16), :] = exponent.astype(jnp.int32).astype(jnp.int16)
        to_sibling.append(send(sib_send.at[k], sib_recv.at[k], moved(me, c=1)))

    def second_half(k):
        zk = (pz + SLAB_ORDER[k]) % 4

        def for_self(i, carry):
            for u in range(UNROLL):
                n = UNROLL * i + u
                x, y, p = n // 8, (n // 2) % 4, n % 2
                owner = ((x * 4 + zk) * 2 + pc) * 4 + y
                acc[x, zk, y, pl.ds(p * SIDE, SIDE), :] = two_blocks(2 * owner + p)
            return carry

        lax.fori_loop(0, 32 // UNROLL, for_self, 0)

    def join(k):
        step = SLAB_ORDER[k]
        zk = (pz + step) % 4
        to_sibling[k].wait_recv()
        scale = jnp.exp2(splat(sib_recv[k, pl.ds(2048, 16), :]))
        top = jnp.zeros((8, 128), F32)
        for x in range(4):
            for y in range(4):
                total = acc[x, zk, y] + scale * sib_recv[k, pl.ds((x * 4 + y) * 128, 128), :].astype(F32)
                acc[x, zk, y] = total
                top = jnp.maximum(top, jnp.max(jnp.abs(total).reshape(16, 8, 128), axis=0))
        exponent = exponent_of(top)
        inverse = jnp.exp2(-exponent)[0:1, :]
        exponent = exponent.astype(jnp.int32).astype(jnp.int16)
        slab = []
        if step:
            for x in range(4):
                for y in range(4):
                    send1c[step - 1, pl.ds((x * 4 + y) * 32, 32), :] = encode(acc[x, zk, y, 96:128, :], inverse)
            send1c[step - 1, pl.ds(512, 16), :] = exponent
            slab.append(send(send1c.at[step - 1], recv1c.at[step - 1], moved(me, z=step)))
        for d in (2, 1, 3):
            to = (px + d) % 4
            for y in range(4):
                send1a[k, d - 1, pl.ds(y * 48, 48), :] = encode(acc[to, zk, y, 0:48, :], inverse)
            send1a[k, d - 1, pl.ds(192, 16), :] = exponent
            slab.append(send(send1a.at[k, d - 1], recv1a.at[k, d - 1], moved(me, x=d)))
            to = (py + d) % 4
            for x in range(4):
                send1b[k, d - 1, pl.ds(x * 48, 48), :] = encode(acc[x, zk, to, 48:96, :], inverse)
            send1b[k, d - 1, pl.ds(192, 16), :] = exponent
            slab.append(send(send1b.at[k, d - 1], recv1b.at[k, d - 1], moved(me, y=d)))
        sends1.append(slab)

    first_half(0)
    state_copies = swap_state()
    for k in range(4):
        second_half(k)
        if k < 3:
            first_half(k + 1)
        join(k)

    def finish(k):
        step = SLAB_ORDER[k]
        zk = (pz + step) % 4
        slab = list(sends1[k])
        if step:
            slab.pop(0).wait_recv()
            scale = jnp.exp2(splat(recv1c[step - 1, pl.ds(512, 16), :]))
            for x in range(4):
                for y in range(4):
                    acc[x, pz, y, 96:128, :] += scale * recv1c[step - 1, pl.ds((x * 4 + y) * 32, 32), :].astype(F32)
        for n, d in enumerate((2, 1, 3)):
            slab[2 * n].wait_recv()
            scale = jnp.exp2(splat(recv1a[k, d - 1, pl.ds(192, 16), :]))
            for y in range(4):
                acc[px, zk, y, 0:48, :] += scale * recv1a[k, d - 1, pl.ds(y * 48, 48), :].astype(F32)
            slab[2 * n + 1].wait_recv()
            scale = jnp.exp2(splat(recv1b[k, d - 1, pl.ds(192, 16), :]))
            for x in range(4):
                acc[x, zk, py, 48:96, :] += scale * recv1b[k, d - 1, pl.ds(x * 48, 48), :].astype(F32)

    for k in range(4):
        finish(k)

    def later_phase(axis, out_buf, in_buf, rows, first, count, place):
        held = [[acc[(*place(j, (me[axis] + d) % 4), pl.ds(first, rows), slice(None))] for j in range(count)] for d in (2, 1, 3)]
        top = functools.reduce(jnp.maximum, [jnp.max(jnp.abs(v).reshape(rows // 8, 8, 128), axis=0) for h in held for v in h])
        exponent = exponent_of(top)
        inverse = jnp.exp2(-exponent)[0:1, :]
        exponent = exponent.astype(jnp.int32).astype(jnp.int16)
        copies = []
        for h, d in zip(held, (2, 1, 3), strict=True):
            for j, v in enumerate(h):
                out_buf[d - 1, pl.ds(j * rows, rows), :] = encode(v, inverse)
            out_buf[d - 1, pl.ds(count * rows, 16), :] = exponent
            copies.append(send(out_buf.at[d - 1], in_buf.at[d - 1], moved(me, **{axis: d})))

        def add():
            for d, copy in zip((2, 1, 3), copies, strict=True):
                copy.wait_recv()
                scale = jnp.exp2(splat(in_buf[d - 1, pl.ds(count * rows, 16), :]))
                for j in range(count):
                    acc[(*place(j, me[axis]), pl.ds(first, rows), slice(None))] += scale * in_buf[d - 1, pl.ds(j * rows, rows), :].astype(F32)

        return add

    adds = [
        later_phase("x", send2c, recv2c, 32, 96, 4, lambda j, q: (q, pz, j)),
        later_phase("y", send2a, recv2a, 48, 0, 4, lambda j, q: (px, j, q)),
        later_phase("z", send2b, recv2b, 48, 48, 4, lambda j, q: (j, q, py)),
    ]
    adds[0]()
    last = [later_phase("y", send3c, recv3c, 32, 96, 1, lambda j, q: (px, pz, q))]
    adds[1]()
    last.append(later_phase("z", send3a, recv3a, 48, 0, 1, lambda j, q: (px, q, py)))
    adds[2]()
    last.append(later_phase("x", send3b, recv3b, 48, 48, 1, lambda j, q: (q, pz, py)))
    for add in last:
        add()

    counts = live_ref[0:1, :].astype(F32)
    owner = ((px * 4 + pz) * 2 + pc) * 4 + py
    at = lax.broadcasted_iota(jnp.int32, (1, 128), 1)
    mine = jnp.sum(jnp.where(at == owner, counts, 0.0))
    live_total = jnp.sum(counts) * float(SIDE * SIDE)
    slot = 2 * (lax.broadcasted_iota(jnp.int32, (128, 128), 0) // SIDE) + lax.broadcasted_iota(jnp.int32, (128, 128), 1) // SIDE
    own = jnp.where(slot.astype(F32) < mine, acc[px, pz, py], 0.0)
    sum_send[0] = jnp.full((8, 128), jnp.sum(own * own), F32)
    copies = []
    for n, by in enumerate([{"c": 1}] + [{"x": d, "c": c} for d in (1, 2, 3) for c in (0, 1)]):
        copies.append(send(sum_send.at[0], sum_recv.at[n], moved(me, **by)))
    turned[...] = own.T
    even, odd = turned[pl.ds(0, SIDE, 2), :], turned[pl.ds(1, SIDE, 2), :]
    flat[pl.ds(0, SIDE), :] = jnp.where(lane < SIDE, even, pltpu.roll(odd, SIDE, 1))
    flat[pl.ds(SIDE, SIDE), :] = jnp.where(lane < SIDE, pltpu.roll(even, SIDE, 1), odd)
    for t in range(32):
        to, part = part_of(t)
        swap_send[to, part // 2, pl.ds(4 * (part % 2), 4), :] = flat[pl.ds(t, 4, 32), :]
    swaps = [send(swap_send.at[(py + d) % 4], swap_recv.at[py], moved(me, y=d)) for d in (2, 1, 3)]
    swap_recv[py] = swap_send[py]
    square = sum_send[0]
    for n, copy in enumerate(copies):
        copy.wait_recv()
        square += sum_recv[n]
    sum_send[1] = square
    copies = []
    for i in range(4):
        for j in range(4):
            if i or j:
                copies.append(send(sum_send.at[1], sum_recv.at[7 + len(copies)], moved(me, y=i, z=j)))
    for n, copy in enumerate(copies):
        copy.wait_recv()
        square += sum_recv[7 + n]
    for copy in swaps + state_copies:
        copy.wait_recv()
    mean_square = square / live_total
    clip = jnp.minimum(1.0, 1.0 / jnp.sqrt(mean_square + 1e-06))

    for part in range(8):
        for source in range(4):
            rows, at = pl.ds(4 * source, 4), pl.ds(4 * (part % 2), 4)
            joined[3, part, rows, :] = swap_recv[source, part // 2, at, :]
            for n in range(3):
                joined[n, part, rows, :] = state_recv[source, n, part // 2, at, :]
    part = 0
    for first, width in GATHER:
        for column in range(0, width, 128):
            at = pl.multiple_of(first + column + py * width, 128)
            new_master, _, _ = adamw(clip[0:1] * joined[3, part], joined[0, part], joined[1, part], joined[2, part])
            held[px, pz, :, pl.ds(at, 128)] = new_master.astype(jnp.bfloat16)
            part += 1

    def spread(n, fixed, axis):
        part = region(held, n, fixed)
        return {d: send(part, part, moved(me, **{axis: d})) for d in (2, 1, 3)}

    orders = [order for _, _, order in STREAMS]
    inner = [spread(n, {"x": px, "y": py, "z": pz}, order[2]) for n, order in enumerate(orders)]
    for t in range(32):
        at = pl.ds(t * 128, 128)
        clipped = clip[0:4] * flat[pl.ds(t, 4, 32), :]
        new_master, new_moment, new_variance = adamw(clipped, master_ref[:, at], moment_ref[:, at], variance_ref[:, at])
        clipped_ref[:, at] = clipped
        new_moment_ref[:, at] = new_moment
        new_variance_ref[:, at] = new_variance
        new_master_ref[:, at] = new_master
    stores = []

    def store(src, dst):
        copy = pltpu.make_async_copy(src, dst, store_sem.at[len(stores)])
        copy.start()
        stores.append(copy)

    store(new_master_ref, new_master_hbm)
    store(new_moment_ref, new_moment_hbm)
    store(new_variance_ref, new_variance_hbm)
    store(clipped_ref, clipped_hbm)
    middle, outer = [], []
    for n, order in enumerate(orders):
        for copy in inner[n].values():
            copy.wait_recv()
        middle.append(spread(n, {a: me[a] for a in order[:2]}, order[1]))
    for n, order in enumerate(orders):
        outer.append([spread(n, {a: me[a] for a in order[:2]}, order[0])])
    for d in (1, 3, 2):
        for n, order in enumerate(orders):
            middle[n][d].wait_recv()
            outer[n].append(spread(n, {order[0]: me[order[0]], order[1]: (me[order[1]] - d) % 4}, order[0]))
    other = moved(me, c=1)
    passed = []

    def settle(n, fixed):
        part, place = region(held, n, fixed), region(published, n, fixed, pc)
        passed.append(send(part, place, other))
        store(part, place)

    for n, order in enumerate(orders):
        settle(n, {order[0]: me[order[0]]})
    for d in (1, 3):
        for n, order in enumerate(orders):
            for piece in outer[n]:
                piece[d].wait_recv()
            settle(n, {order[0]: (me[order[0]] - d) % 4})
    for m, e in enumerate((0, 1, 3, 2)):
        for n, order in enumerate(orders):
            outer[n][m][2].wait_recv()
            settle(n, {order[0]: (me[order[0]] - 2) % 4, order[1]: (me[order[1]] - e) % 4})
    for copy in passed:
        copy.wait_recv()
    for copy in issued:
        copy.wait_send()
    for copy in stores:
        copy.wait()


def pass_on(*refs):
    sources, results, sem = refs[:5], refs[5:10], refs[10]
    copies = []
    for i in range(4):
        rows = pl.ds(i * 128, 128)
        copies.append(pltpu.make_async_copy(sources[4].at[rows], results[4].at[rows], sem.at[i]))
        copies.append(pltpu.make_async_copy(sources[i], results[i], sem.at[4 + i]))
    for copy in copies:
        copy.start()
    for copy in copies:
        copy.wait()


def local(hidden, grad_out, block_list, live_block_count, master, moment, variance):
    i16 = jnp.int16
    state = jax.ShapeDtypeStruct(master.shape, F32)
    vmem, hbm = pl.BlockSpec(memory_space=pltpu.VMEM), pl.BlockSpec(memory_space=pltpu.HBM)
    first = [pltpu.VMEM((4, 3, 208, 128), i16)] * 4 + [pltpu.VMEM((3, 528, 128), i16)] * 2
    second = [pltpu.VMEM((3, 208, 128), i16)] * 4 + [pltpu.VMEM((3, 144, 128), i16)] * 2
    third = [pltpu.VMEM((3, 64, 128), i16)] * 4 + [pltpu.VMEM((3, 48, 128), i16)] * 2
    copies = 4 + 27 + 18 + 22 + 3 + 3 + 9 + 9 + 36 + 21
    *updated, published = pl.pallas_call(
        kernel,
        out_shape=[state] * 4 + [jax.ShapeDtypeStruct((4, 4, 2, 16, 4096), jnp.bfloat16)],
        in_specs=[hbm] * 7,
        out_specs=[hbm] * 5,
        scratch_shapes=[
            pltpu.SMEM(block_list.shape[::-1], jnp.int32),
            pltpu.VMEM(hidden.shape, jnp.bfloat16),
            pltpu.VMEM(grad_out.shape, jnp.bfloat16),
            pltpu.VMEM(grad_out.shape[::-1], jnp.bfloat16),
            pltpu.VMEM((1, live_block_count.shape[0]), jnp.int32),
            *[pltpu.VMEM(master.shape, F32)] * 7,
            pltpu.VMEM((4, 4, 4, 128, 128), F32),
            pltpu.VMEM((4, 4, 128, 128), F32),
            pltpu.VMEM((4, 2064, 128), i16),
            pltpu.VMEM((4, 2064, 128), i16),
            *first, *second, *third,
            pltpu.VMEM((128, 128), F32),
            pltpu.VMEM((128, 128), F32),
            pltpu.VMEM((2, 8, 128), F32),
            pltpu.VMEM((22, 8, 128), F32),
            pltpu.VMEM((4, 4, 8, 128), F32),
            pltpu.VMEM((4, 4, 8, 128), F32),
            pltpu.VMEM((4, 3, 4, 8, 128), F32),
            pltpu.VMEM((4, 3, 4, 8, 128), F32),
            pltpu.VMEM((4, 8, 16, 128), F32),
            pltpu.VMEM((4, 4, 16, 4096), jnp.bfloat16),
            pltpu.SemaphoreType.DMA((7,)),
            pltpu.SemaphoreType.DMA((25,)),
            pltpu.SemaphoreType.DMA((copies,)),
            pltpu.SemaphoreType.DMA((copies,)),
        ],
        compiler_params=pltpu.CompilerParams(
            collective_id=0, has_side_effects=True, vmem_limit_bytes=30 * 2**20
        ),
    )(
        *[pltpu.with_memory_space_constraint(a, pltpu.HBM) for a in (block_list.T, hidden, grad_out, live_block_count.reshape(1, -1), master, moment, variance)],
    )
    return pl.pallas_call(
        pass_on,
        out_shape=[state] * 4 + [jax.ShapeDtypeStruct((512, 4096), jnp.bfloat16)],
        in_specs=[hbm] * 5,
        out_specs=[hbm] * 5,
        scratch_shapes=[pltpu.SemaphoreType.DMA((8,))],
        compiler_params=pltpu.CompilerParams(vmem_limit_bytes=2**20),
    )(*updated, published.reshape(512, 4096))


def solution(mesh):
    one, all_of_it = P(("dp", "owner"), None), P()
    return jax.shard_map(
        local,
        mesh=mesh,
        in_specs=(one, one, all_of_it, all_of_it, one, one, one),
        out_specs=(one, one, one, one, all_of_it),
        check_vma=False,
    )
```

```python
import functools

import jax
import jax.numpy as jnp
from jax import lax
from jax.experimental import pallas as pl
from jax.experimental.pallas import tpu as pltpu
from jax.sharding import PartitionSpec as P

MESH = pl.DeviceIdType.MESH
SIDE = 64
UNROLL = 32
SLAB_ORDER = (2, 1, 3, 0)
STREAMS = ((0, 48, "xyz"), (48, 48, "yzx"), (96, 32, "zxy"))
F32 = jnp.float32


def where_am_i():
    dp = lax.axis_index("dp")
    y = lax.axis_index("owner")
    return {"x": dp // 8, "z": (dp // 2) % 4, "c": dp % 2, "y": y}


def device_at(place):
    return ((place["x"] * 4 + place["z"]) * 2 + place["c"], place["y"])


def moved(me, **by):
    place = dict(me)
    for axis, step in by.items():
        place[axis] = (me[axis] + step) % (2 if axis == "c" else 4)
    return place


def exponent_of(top):
    top = jnp.maximum(jnp.full((16, 128), jnp.max(top), F32), 1e-30)
    return jnp.ceil(jnp.log2(top * (1.0 / 32000.0)))


def encode(values, inverse):
    return jnp.round(values * inverse).astype(jnp.int32).astype(jnp.int16)


def splat(tile):
    return tile[0:1, :].astype(F32)


GATHER = ((0, 384), (1536, 384), (3072, 256))


def region(buf, n, fixed, core=None):
    first, width = GATHER[n]
    start, size = (first + fixed["y"] * width, width) if "y" in fixed else (first, 4 * width)
    index = [fixed.get(a, slice(None)) for a in "xz"] + ([] if core is None else [core])
    return buf.at[(*index, slice(None), pl.ds(start, size))]


def part_of(t):
    to, part = divmod(t, 3) if t < 12 else divmod(t - 12, 3) if t < 24 else divmod(t - 24, 2)
    return to, part + (0 if t < 12 else 3 if t < 24 else 6)


def adamw(clipped, master, moment, variance):
    new_moment = 0.9 * moment + 0.1 * clipped
    new_variance = 0.95 * variance + 0.05 * clipped * clipped
    moment_hat = new_moment / (1.0 - 0.9**20)
    variance_hat = new_variance / (1.0 - 0.95**20)
    new_master = master - 0.02 * (moment_hat / (jnp.sqrt(variance_hat) + 1e-08) + 0.1 * master)
    return new_master, new_moment, new_variance


def kernel(
    list_hbm, hidden_hbm, grad_out_hbm, live_hbm, master_hbm, moment_hbm, variance_hbm,
    new_master_hbm, new_moment_hbm, new_variance_hbm, clipped_hbm, published,
    list_ref, hidden, grad_out, grad_out_t, live_ref, master_ref, moment_ref, variance_ref,
    new_master_ref, new_moment_ref, new_variance_ref, clipped_ref, acc, pair_part, sib_send, sib_recv,
    send1a, recv1a, send1b, recv1b, send1c, recv1c,
    send2a, recv2a, send2b, recv2b, send2c, recv2c,
    send3a, recv3a, send3b, recv3b, send3c, recv3c,
    turned, flat, sum_send, sum_recv, swap_send, swap_recv, state_send, state_recv, joined, held,
    load_sem, store_sem, send_sem, recv_sem,
):
    me = where_am_i()
    px, py, pz, pc = me["x"], me["y"], me["z"], me["c"]
    peers = [moved(me, c=1)]
    peers += [moved(me, **{a: d}) for a in "xyz" for d in (1, 2, 3)]
    peers += [moved(me, x=d, c=1) for d in (1, 2, 3)]
    peers += [moved(me, y=i, z=j) for i in (1, 2, 3) for j in (1, 2, 3)]
    barrier = pltpu.get_barrier_semaphore()
    for peer in peers:
        pl.semaphore_signal(barrier, inc=1, device_id=device_at(peer), device_id_type=MESH)

    loads = [
        pltpu.make_async_copy(grad_out_hbm, grad_out, load_sem.at[0]),
        pltpu.make_async_copy(hidden_hbm, hidden, load_sem.at[1]),
        pltpu.make_async_copy(list_hbm, list_ref, load_sem.at[6]),
        pltpu.make_async_copy(live_hbm, live_ref, load_sem.at[2]),
        pltpu.make_async_copy(master_hbm, master_ref, load_sem.at[3]),
        pltpu.make_async_copy(moment_hbm, moment_ref, load_sem.at[4]),
        pltpu.make_async_copy(variance_hbm, variance_ref, load_sem.at[5]),
    ]
    for load in loads:
        load.start()

    loads[0].wait()
    for t in range(20):
        grad_out_t[pl.ds(t * 128, 128), :] = grad_out[:, t * 128 : (t + 1) * 128].T
    loads[1].wait()
    loads[2].wait()
    pl.semaphore_wait(barrier, len(peers))

    issued = []

    def send(src, dst, to):
        n = len(issued)
        copy = pltpu.make_async_remote_copy(
            src_ref=src, dst_ref=dst, send_sem=send_sem.at[n], recv_sem=recv_sem.at[n],
            device_id=device_at(to), device_id_type=MESH,
        )
        copy.start()
        issued.append(copy)
        return copy

    lane = lax.broadcasted_iota(jnp.int32, (SIDE, 128), 1)

    low = lane < SIDE

    def two_blocks(pair):
        both, odd = [], []
        for slot in (2 * pair, 2 * pair + 1):
            row, column = list_ref[0, slot], list_ref[1, slot]
            left = grad_out_t[pl.ds(column * SIDE, SIDE), :]
            right = hidden[:, pl.ds((row >> 1) * 128, 128)]
            both.append(jnp.dot(left, right, preferred_element_type=F32))
            odd.append(row & 1)
        crossed = pltpu.roll(jnp.where(low, both[1], both[0]), SIDE, 1)
        straight = jnp.where(low, both[0], both[1])
        return jnp.where(jnp.where(low, odd[0], 1 - odd[1]) == 1, crossed, straight)

    def swap_state():
        for load in loads[3:]:
            load.wait()
        for n, ref in enumerate((master_ref, moment_ref, variance_ref)):
            for t in range(32):
                to, part = part_of(t)
                state_send[to, n, part // 2, pl.ds(4 * (part % 2), 4), :] = ref[:, t * 128 : (t + 1) * 128]
        state_recv[py] = state_send[py]
        return [send(state_send.at[(py + d) % 4], state_recv.at[py], moved(me, y=d)) for d in (2, 1, 3)]

    sends1, to_sibling = [], []

    def first_half(k):
        zk = (pz + SLAB_ORDER[k]) % 4

        def for_sibling(i, top):
            for u in range(UNROLL):
                n = UNROLL * i + u
                x, y, p = n // 8, (n // 2) % 4, n % 2
                owner = ((x * 4 + zk) * 2 + (1 - pc)) * 4 + y
                part = two_blocks(2 * owner + p)
                pair_part[x, y, pl.ds(p * SIDE, SIDE), :] = part
                top = jnp.maximum(top, jnp.max(jnp.abs(part).reshape(8, 8, 128), axis=0))
            return top

        top = lax.fori_loop(0, 32 // UNROLL, for_sibling, jnp.zeros((8, 128), F32))
        exponent = exponent_of(top)
        inverse = jnp.exp2(-exponent)[0:1, :]
        for x in range(4):
            for y in range(4):
                sib_send[k, pl.ds((x * 4 + y) * 128, 128), :] = encode(pair_part[x, y], inverse)
        sib_send[k, pl.ds(2048, 16), :] = exponent.astype(jnp.int32).astype(jnp.int16)
        to_sibling.append(send(sib_send.at[k], sib_recv.at[k], moved(me, c=1)))

    def second_half(k):
        zk = (pz + SLAB_ORDER[k]) % 4

        def for_self(i, carry):
            for u in range(UNROLL):
                n = UNROLL * i + u
                x, y, p = n // 8, (n // 2) % 4, n % 2
                owner = ((x * 4 + zk) * 2 + pc) * 4 + y
                acc[x, zk, y, pl.ds(p * SIDE, SIDE), :] = two_blocks(2 * owner + p)
            return carry

        lax.fori_loop(0, 32 // UNROLL, for_self, 0)

    def join(k):
        step = SLAB_ORDER[k]
        zk = (pz + step) % 4
        to_sibling[k].wait_recv()
        scale = jnp.exp2(splat(sib_recv[k, pl.ds(2048, 16), :]))
        top = jnp.zeros((8, 128), F32)
        for x in range(4):
            for y in range(4):
                total = acc[x, zk, y] + scale * sib_recv[k, pl.ds((x * 4 + y) * 128, 128), :].astype(F32)
                acc[x, zk, y] = total
                top = jnp.maximum(top, jnp.max(jnp.abs(total).reshape(16, 8, 128), axis=0))
        exponent = exponent_of(top)
        inverse = jnp.exp2(-exponent)[0:1, :]
        exponent = exponent.astype(jnp.int32).astype(jnp.int16)
        slab = []
        if step:
            for x in range(4):
                for y in range(4):
                    send1c[step - 1, pl.ds((x * 4 + y) * 32, 32), :] = encode(acc[x, zk, y, 96:128, :], inverse)
            send1c[step - 1, pl.ds(512, 16), :] = exponent
            slab.append(send(send1c.at[step - 1], recv1c.at[step - 1], moved(me, z=step)))
        for d in (2, 1, 3):
            to = (px + d) % 4
            for y in range(4):
                send1a[k, d - 1, pl.ds(y * 48, 48), :] = encode(acc[to, zk, y, 0:48, :], inverse)
            send1a[k, d - 1, pl.ds(192, 16), :] = exponent
            slab.append(send(send1a.at[k, d - 1], recv1a.at[k, d - 1], moved(me, x=d)))
            to = (py + d) % 4
            for x in range(4):
                send1b[k, d - 1, pl.ds(x * 48, 48), :] = encode(acc[x, zk, to, 48:96, :], inverse)
            send1b[k, d - 1, pl.ds(192, 16), :] = exponent
            slab.append(send(send1b.at[k, d - 1], recv1b.at[k, d - 1], moved(me, y=d)))
        sends1.append(slab)

    first_half(0)
    state_copies = swap_state()
    for k in range(4):
        second_half(k)
        if k < 3:
            first_half(k + 1)
        join(k)

    def finish(k):
        step = SLAB_ORDER[k]
        zk = (pz + step) % 4
        slab = list(sends1[k])
        if step:
            slab.pop(0).wait_recv()
            scale = jnp.exp2(splat(recv1c[step - 1, pl.ds(512, 16), :]))
            for x in range(4):
                for y in range(4):
                    acc[x, pz, y, 96:128, :] += scale * recv1c[step - 1, pl.ds((x * 4 + y) * 32, 32), :].astype(F32)
        for n, d in enumerate((2, 1, 3)):
            slab[2 * n].wait_recv()
            scale = jnp.exp2(splat(recv1a[k, d - 1, pl.ds(192, 16), :]))
            for y in range(4):
                acc[px, zk, y, 0:48, :] += scale * recv1a[k, d - 1, pl.ds(y * 48, 48), :].astype(F32)
            slab[2 * n + 1].wait_recv()
            scale = jnp.exp2(splat(recv1b[k, d - 1, pl.ds(192, 16), :]))
            for x in range(4):
                acc[x, zk, py, 48:96, :] += scale * recv1b[k, d - 1, pl.ds(x * 48, 48), :].astype(F32)

    for k in range(4):
        finish(k)

    def later_phase(axis, out_buf, in_buf, rows, first, count, place):
        held = [[acc[(*place(j, (me[axis] + d) % 4), pl.ds(first, rows), slice(None))] for j in range(count)] for d in (2, 1, 3)]
        top = functools.reduce(jnp.maximum, [jnp.max(jnp.abs(v).reshape(rows // 8, 8, 128), axis=0) for h in held for v in h])
        exponent = exponent_of(top)
        inverse = jnp.exp2(-exponent)[0:1, :]
        exponent = exponent.astype(jnp.int32).astype(jnp.int16)
        copies = []
        for h, d in zip(held, (2, 1, 3), strict=True):
            for j, v in enumerate(h):
                out_buf[d - 1, pl.ds(j * rows, rows), :] = encode(v, inverse)
            out_buf[d - 1, pl.ds(count * rows, 16), :] = exponent
            copies.append(send(out_buf.at[d - 1], in_buf.at[d - 1], moved(me, **{axis: d})))

        def add():
            for d, copy in zip((2, 1, 3), copies, strict=True):
                copy.wait_recv()
                scale = jnp.exp2(splat(in_buf[d - 1, pl.ds(count * rows, 16), :]))
                for j in range(count):
                    acc[(*place(j, me[axis]), pl.ds(first, rows), slice(None))] += scale * in_buf[d - 1, pl.ds(j * rows, rows), :].astype(F32)

        return add

    adds = [
        later_phase("x", send2c, recv2c, 32, 96, 4, lambda j, q: (q, pz, j)),
        later_phase("y", send2a, recv2a, 48, 0, 4, lambda j, q: (px, j, q)),
        later_phase("z", send2b, recv2b, 48, 48, 4, lambda j, q: (j, q, py)),
    ]
    adds[0]()
    last = [later_phase("y", send3c, recv3c, 32, 96, 1, lambda j, q: (px, pz, q))]
    adds[1]()
    last.append(later_phase("z", send3a, recv3a, 48, 0, 1, lambda j, q: (px, q, py)))
    adds[2]()
    last.append(later_phase("x", send3b, recv3b, 48, 48, 1, lambda j, q: (q, pz, py)))
    counts = live_ref[0:1, :].astype(F32)
    owner = ((px * 4 + pz) * 2 + pc) * 4 + py
    at = lax.broadcasted_iota(jnp.int32, (1, 128), 1)
    mine = jnp.sum(jnp.where(at == owner, counts, 0.0))
    live_total = jnp.sum(counts) * float(SIDE * SIDE)
    slot = 2 * (lax.broadcasted_iota(jnp.int32, (128, 128), 0) // SIDE) + lax.broadcasted_iota(jnp.int32, (128, 128), 1) // SIDE
    live = slot.astype(F32) < mine
    for add in last:
        add()

    own = jnp.where(live, acc[px, pz, py], 0.0)
    sum_send[0] = jnp.full((1, 128), jnp.sum(own * own), F32)
    copies = []
    for n, by in enumerate([{"c": 1}] + [{"x": d, "c": c} for d in (1, 2, 3) for c in (0, 1)]):
        copies.append(send(sum_send.at[0], sum_recv.at[n], moved(me, **by)))
    turned[...] = own.T
    even, odd = turned[pl.ds(0, SIDE, 2), :], turned[pl.ds(1, SIDE, 2), :]
    flat[pl.ds(0, SIDE), :] = jnp.where(lane < SIDE, even, pltpu.roll(odd, SIDE, 1))
    flat[pl.ds(SIDE, SIDE), :] = jnp.where(lane < SIDE, pltpu.roll(even, SIDE, 1), odd)
    for t in range(32):
        to, part = part_of(t)
        swap_send[to, part // 2, pl.ds(4 * (part % 2), 4), :] = flat[pl.ds(t, 4, 32), :]
    swaps = [send(swap_send.at[(py + d) % 4], swap_recv.at[py], moved(me, y=d)) for d in (2, 1, 3)]
    swap_recv[py] = swap_send[py]
    square = sum_send[0]
    for n, copy in enumerate(copies):
        copy.wait_recv()
        square += sum_recv[n]
    sum_send[1] = square
    copies = []
    for i in range(4):
        for j in range(4):
            if i or j:
                copies.append(send(sum_send.at[1], sum_recv.at[7 + len(copies)], moved(me, y=i, z=j)))
    for n, copy in enumerate(copies):
        copy.wait_recv()
        square += sum_recv[7 + n]
    for copy in swaps + state_copies:
        copy.wait_recv()
    mean_square = square / live_total
    clip = jnp.minimum(1.0, 1.0 / jnp.sqrt(mean_square + 1e-06))

    for part in range(8):
        for source in range(4):
            rows, at = pl.ds(4 * source, 4), pl.ds(4 * (part % 2), 4)
            joined[3, part, rows, :] = swap_recv[source, part // 2, at, :]
            for n in range(3):
                joined[n, part, rows, :] = state_recv[source, n, part // 2, at, :]
    part = 0
    for first, width in GATHER:
        for column in range(0, width, 128):
            at = pl.multiple_of(first + column + py * width, 128)
            new_master, _, _ = adamw(clip[0:1] * joined[3, part], joined[0, part], joined[1, part], joined[2, part])
            held[px, pz, :, pl.ds(at, 128)] = new_master.astype(jnp.bfloat16)
            part += 1

    def spread(n, fixed, axis, steps=(2, 1, 3)):
        part = region(held, n, fixed)
        return {d: send(part, part, moved(me, **{axis: d})) for d in steps}

    orders = [order for _, _, order in STREAMS]
    inner = [spread(n, {"x": px, "y": py, "z": pz}, order[2]) for n, order in enumerate(orders)]
    for t in range(32):
        at = pl.ds(t * 128, 128)
        clipped = clip * flat[pl.ds(t, 4, 32), :]
        new_master, new_moment, new_variance = adamw(clipped, master_ref[:, at], moment_ref[:, at], variance_ref[:, at])
        clipped_ref[:, at] = clipped
        new_moment_ref[:, at] = new_moment
        new_variance_ref[:, at] = new_variance
        new_master_ref[:, at] = new_master
    stores = []

    def store(src, dst):
        copy = pltpu.make_async_copy(src, dst, store_sem.at[len(stores)])
        copy.start()
        stores.append(copy)

    store(new_master_ref, new_master_hbm)
    store(new_moment_ref, new_moment_hbm)
    store(new_variance_ref, new_variance_hbm)
    store(clipped_ref, clipped_hbm)
    middle = []
    for n, order in enumerate(orders):
        for copy in inner[n].values():
            copy.wait_recv()
        middle.append(spread(n, {a: me[a] for a in order[:2]}, order[1]))
    turns = (0, 1, 3, 2)
    outer, beyond = [[] for _ in orders], [{} for _ in orders]

    def outward(m):
        for n, order in enumerate(orders):
            if m:
                middle[n][turns[m]].wait_recv()
            fixed = {order[0]: me[order[0]], order[1]: (me[order[1]] - turns[m]) % 4}
            outer[n].append(spread(n, fixed, order[0], (1, 3)))

    def onward(m):
        d = 1 if m < 2 else 3
        for n, order in enumerate(orders):
            outer[n][m].pop(d).wait_recv()
            fixed = {order[0]: (me[order[0]] - d) % 4, order[1]: (me[order[1]] - turns[m]) % 4}
            beyond[n].update({m: spread(n, fixed, order[0], (d,))[d]})

    outward(0)
    outward(1)
    onward(0)
    outward(2)
    outward(3)
    for m in (1, 2, 3):
        onward(m)
    other = moved(me, c=1)
    passed = []

    def settle(n, fixed):
        part, place = region(held, n, fixed), region(published, n, fixed, pc)
        passed.append(send(part, place, other))
        store(part, place)

    for n, order in enumerate(orders):
        settle(n, {order[0]: me[order[0]]})
    for d in (1, 3):
        for n, order in enumerate(orders):
            for piece in outer[n]:
                if d in piece:
                    piece[d].wait_recv()
            settle(n, {order[0]: (me[order[0]] - d) % 4})
    for m in range(4):
        for n, order in enumerate(orders):
            beyond[n][m].wait_recv()
            settle(n, {order[0]: (me[order[0]] - 2) % 4, order[1]: (me[order[1]] - turns[m]) % 4})
    for copy in passed:
        copy.wait_recv()
    for copy in issued:
        copy.wait_send()
    for copy in stores:
        copy.wait()


def pass_on(*refs):
    sources, results, sem = refs[:5], refs[5:10], refs[10]
    copies = []
    for i in range(4):
        rows = pl.ds(i * 128, 128)
        copies.append(pltpu.make_async_copy(sources[4].at[rows], results[4].at[rows], sem.at[i]))
        copies.append(pltpu.make_async_copy(sources[i], results[i], sem.at[4 + i]))
    for copy in copies:
        copy.start()
    for copy in copies:
        copy.wait()


def local(hidden, grad_out, block_list, live_block_count, master, moment, variance):
    i16 = jnp.int16
    state = jax.ShapeDtypeStruct(master.shape, F32)
    vmem, hbm = pl.BlockSpec(memory_space=pltpu.VMEM), pl.BlockSpec(memory_space=pltpu.HBM)
    first = [pltpu.VMEM((4, 3, 208, 128), i16)] * 4 + [pltpu.VMEM((3, 528, 128), i16)] * 2
    second = [pltpu.VMEM((3, 208, 128), i16)] * 4 + [pltpu.VMEM((3, 144, 128), i16)] * 2
    third = [pltpu.VMEM((3, 64, 128), i16)] * 4 + [pltpu.VMEM((3, 48, 128), i16)] * 2
    copies = 4 + 27 + 18 + 22 + 3 + 3 + 9 + 9 + 36 + 21
    *updated, published = pl.pallas_call(
        kernel,
        out_shape=[state] * 4 + [jax.ShapeDtypeStruct((4, 4, 2, 16, 4096), jnp.bfloat16)],
        in_specs=[hbm] * 7,
        out_specs=[hbm] * 5,
        scratch_shapes=[
            pltpu.SMEM(block_list.shape[::-1], jnp.int32),
            pltpu.VMEM(hidden.shape, jnp.bfloat16),
            pltpu.VMEM(grad_out.shape, jnp.bfloat16),
            pltpu.VMEM(grad_out.shape[::-1], jnp.bfloat16),
            pltpu.VMEM((1, live_block_count.shape[0]), jnp.int32),
            *[pltpu.VMEM(master.shape, F32)] * 7,
            pltpu.VMEM((4, 4, 4, 128, 128), F32),
            pltpu.VMEM((4, 4, 128, 128), F32),
            pltpu.VMEM((4, 2064, 128), i16),
            pltpu.VMEM((4, 2064, 128), i16),
            *first, *second, *third,
            pltpu.VMEM((128, 128), F32),
            pltpu.VMEM((128, 128), F32),
            pltpu.VMEM((2, 1, 128), F32),
            pltpu.VMEM((22, 1, 128), F32),
            pltpu.VMEM((4, 4, 8, 128), F32),
            pltpu.VMEM((4, 4, 8, 128), F32),
            pltpu.VMEM((4, 3, 4, 8, 128), F32),
            pltpu.VMEM((4, 3, 4, 8, 128), F32),
            pltpu.VMEM((4, 8, 16, 128), F32),
            pltpu.VMEM((4, 4, 16, 4096), jnp.bfloat16),
            pltpu.SemaphoreType.DMA((7,)),
            pltpu.SemaphoreType.DMA((25,)),
            pltpu.SemaphoreType.DMA((copies,)),
            pltpu.SemaphoreType.DMA((copies,)),
        ],
        compiler_params=pltpu.CompilerParams(
            collective_id=0, has_side_effects=True, vmem_limit_bytes=30 * 2**20
        ),
    )(
        *[pltpu.with_memory_space_constraint(a, pltpu.HBM) for a in (block_list.T, hidden, grad_out, live_block_count.reshape(1, -1), master, moment, variance)],
    )
    return pl.pallas_call(
        pass_on,
        out_shape=[state] * 4 + [jax.ShapeDtypeStruct((512, 4096), jnp.bfloat16)],
        in_specs=[hbm] * 5,
        out_specs=[hbm] * 5,
        scratch_shapes=[pltpu.SemaphoreType.DMA((8,))],
        compiler_params=pltpu.CompilerParams(vmem_limit_bytes=2**20),
    )(*updated, published.reshape(512, 4096))


def solution(mesh):
    one, all_of_it = P(("dp", "owner"), None), P()
    return jax.shard_map(
        local,
        mesh=mesh,
        in_specs=(one, one, all_of_it, all_of_it, one, one, one),
        out_specs=(one, one, one, one, all_of_it),
        check_vma=False,
    )
```

```python
import functools

import jax
import jax.numpy as jnp
from jax import lax
from jax.experimental import pallas as pl
from jax.experimental.pallas import tpu as pltpu
from jax.sharding import PartitionSpec as P

MESH = pl.DeviceIdType.MESH
SIDE = 64
UNROLL = 32
SLAB_ORDER = (2, 1, 3, 0)
STREAMS = ((0, 48, "xyz"), (48, 48, "yzx"), (96, 32, "zxy"))
F32 = jnp.float32


def where_am_i():
    dp = lax.axis_index("dp")
    y = lax.axis_index("owner")
    return {"x": dp // 8, "z": (dp // 2) % 4, "c": dp % 2, "y": y}


def device_at(place):
    return ((place["x"] * 4 + place["z"]) * 2 + place["c"], place["y"])


def moved(me, **by):
    place = dict(me)
    for axis, step in by.items():
        place[axis] = (me[axis] + step) % (2 if axis == "c" else 4)
    return place


def exponent_of(top):
    top = jnp.maximum(jnp.full((16, 128), jnp.max(top), F32), 1e-30)
    return jnp.ceil(jnp.log2(top * (1.0 / 32000.0)))


def encode(values, inverse):
    return jnp.round(values * inverse).astype(jnp.int32).astype(jnp.int16)


def splat(tile):
    return tile[0:1, :].astype(F32)


GATHER = ((0, 384), (1536, 384), (3072, 256))


def region(buf, n, fixed, core=None):
    first, width = GATHER[n]
    start, size = (first + fixed["y"] * width, width) if "y" in fixed else (first, 4 * width)
    index = [fixed.get(a, slice(None)) for a in "xz"] + ([] if core is None else [core])
    return buf.at[(*index, slice(None), pl.ds(start, size))]


def part_of(t):
    to, part = divmod(t, 3) if t < 12 else divmod(t - 12, 3) if t < 24 else divmod(t - 24, 2)
    return to, part + (0 if t < 12 else 3 if t < 24 else 6)


def adamw(clipped, master, moment, variance):
    new_moment = 0.9 * moment + 0.1 * clipped
    new_variance = 0.95 * variance + 0.05 * clipped * clipped
    moment_hat = new_moment / (1.0 - 0.9**20)
    variance_hat = new_variance / (1.0 - 0.95**20)
    new_master = master - 0.02 * (moment_hat / (jnp.sqrt(variance_hat) + 1e-08) + 0.1 * master)
    return new_master, new_moment, new_variance


def kernel(
    list_hbm, hidden_hbm, grad_out_hbm, live_hbm, master_hbm, moment_hbm, variance_hbm,
    new_master_hbm, new_moment_hbm, new_variance_hbm, clipped_hbm, published,
    list_ref, hidden, grad_out, grad_out_t, live_ref, master_ref, moment_ref, variance_ref,
    new_master_ref, new_moment_ref, new_variance_ref, clipped_ref, acc, pair_part, sib_send, sib_recv,
    send1a, recv1a, send1b, recv1b, send1c, recv1c,
    send2a, recv2a, send2b, recv2b, send2c, recv2c,
    send3a, recv3a, send3b, recv3b, send3c, recv3c,
    turned, flat, sum_send, sum_recv, swap_send, swap_recv, state_send, state_recv, joined, held,
    load_sem, store_sem, send_sem, recv_sem,
):
    me = where_am_i()
    px, py, pz, pc = me["x"], me["y"], me["z"], me["c"]
    peers = [moved(me, c=1)]
    peers += [moved(me, **{a: d}) for a in "xyz" for d in (1, 2, 3)]
    peers += [moved(me, x=d, c=1) for d in (1, 2, 3)]
    peers += [moved(me, y=i, z=j) for i in (1, 2, 3) for j in (1, 2, 3)]
    barrier = pltpu.get_barrier_semaphore()
    for peer in peers:
        pl.semaphore_signal(barrier, inc=1, device_id=device_at(peer), device_id_type=MESH)

    loads = [
        pltpu.make_async_copy(hidden_hbm, hidden, load_sem.at[1]),
        pltpu.make_async_copy(list_hbm, list_ref, load_sem.at[6]),
        pltpu.make_async_copy(live_hbm, live_ref, load_sem.at[2]),
        pltpu.make_async_copy(master_hbm, master_ref, load_sem.at[3]),
        pltpu.make_async_copy(moment_hbm, moment_ref, load_sem.at[4]),
        pltpu.make_async_copy(variance_hbm, variance_ref, load_sem.at[5]),
    ]
    quarters = [pl.ds(q * (grad_out.shape[1] // 4), grad_out.shape[1] // 4) for q in range(4)]
    pieces = [pltpu.make_async_copy(grad_out_hbm.at[:, q], grad_out.at[:, q], load_sem.at[7 + i]) for i, q in enumerate(quarters)]
    for load in pieces + loads:
        load.start()

    for t in range(20):
        if t % 5 == 0:
            pieces[t // 5].wait()
        grad_out_t[pl.ds(t * 128, 128), :] = grad_out[:, t * 128 : (t + 1) * 128].T
    loads[0].wait()
    loads[1].wait()
    pl.semaphore_wait(barrier, len(peers))

    issued = []

    def send(src, dst, to):
        n = len(issued)
        copy = pltpu.make_async_remote_copy(
            src_ref=src, dst_ref=dst, send_sem=send_sem.at[n], recv_sem=recv_sem.at[n],
            device_id=device_at(to), device_id_type=MESH,
        )
        copy.start()
        issued.append(copy)
        return copy

    lane = lax.broadcasted_iota(jnp.int32, (SIDE, 128), 1)

    low = lane < SIDE

    def two_blocks(pair):
        both, odd = [], []
        for slot in (2 * pair, 2 * pair + 1):
            row, column = list_ref[0, slot], list_ref[1, slot]
            left = grad_out_t[pl.ds(column * SIDE, SIDE), :]
            right = hidden[:, pl.ds((row >> 1) * 128, 128)]
            both.append(jnp.dot(left, right, preferred_element_type=F32))
            odd.append(row & 1)
        crossed = pltpu.roll(jnp.where(low, both[1], both[0]), SIDE, 1)
        straight = jnp.where(low, both[0], both[1])
        return jnp.where(jnp.where(low, odd[0], 1 - odd[1]) == 1, crossed, straight)

    def swap_state():
        for load in loads[2:]:
            load.wait()
        for n, ref in enumerate((master_ref, moment_ref, variance_ref)):
            for t in range(32):
                to, part = part_of(t)
                state_send[to, n, part // 2, pl.ds(4 * (part % 2), 4), :] = ref[:, t * 128 : (t + 1) * 128]
        state_recv[py] = state_send[py]
        return [send(state_send.at[(py + d) % 4], state_recv.at[py], moved(me, y=d)) for d in (2, 1, 3)]

    sends1, to_sibling = [], []

    def first_half(k):
        zk = (pz + SLAB_ORDER[k]) % 4

        def for_sibling(i, top):
            for u in range(UNROLL):
                n = UNROLL * i + u
                x, y, p = n // 8, (n // 2) % 4, n % 2
                owner = ((x * 4 + zk) * 2 + (1 - pc)) * 4 + y
                part = two_blocks(2 * owner + p)
                pair_part[x, y, pl.ds(p * SIDE, SIDE), :] = part
                top = jnp.maximum(top, jnp.max(jnp.abs(part).reshape(8, 8, 128), axis=0))
            return top

        top = lax.fori_loop(0, 32 // UNROLL, for_sibling, jnp.zeros((8, 128), F32))
        exponent = exponent_of(top)
        inverse = jnp.exp2(-exponent)[0:1, :]
        for x in range(4):
            for y in range(4):
                sib_send[k, pl.ds((x * 4 + y) * 128, 128), :] = encode(pair_part[x, y], inverse)
        sib_send[k, pl.ds(2048, 16), :] = exponent.astype(jnp.int32).astype(jnp.int16)
        to_sibling.append(send(sib_send.at[k], sib_recv.at[k], moved(me, c=1)))

    def second_half(k):
        zk = (pz + SLAB_ORDER[k]) % 4

        def for_self(i, carry):
            for u in range(UNROLL):
                n = UNROLL * i + u
                x, y, p = n // 8, (n // 2) % 4, n % 2
                owner = ((x * 4 + zk) * 2 + pc) * 4 + y
                acc[x, zk, y, pl.ds(p * SIDE, SIDE), :] = two_blocks(2 * owner + p)
            return carry

        lax.fori_loop(0, 32 // UNROLL, for_self, 0)

    def join(k):
        step = SLAB_ORDER[k]
        zk = (pz + step) % 4
        to_sibling[k].wait_recv()
        scale = jnp.exp2(splat(sib_recv[k, pl.ds(2048, 16), :]))
        top = jnp.zeros((8, 128), F32)
        for x in range(4):
            for y in range(4):
                total = acc[x, zk, y] + scale * sib_recv[k, pl.ds((x * 4 + y) * 128, 128), :].astype(F32)
                acc[x, zk, y] = total
                top = jnp.maximum(top, jnp.max(jnp.abs(total).reshape(16, 8, 128), axis=0))
        exponent = exponent_of(top)
        inverse = jnp.exp2(-exponent)[0:1, :]
        exponent = exponent.astype(jnp.int32).astype(jnp.int16)
        slab = []
        if step:
            for x in range(4):
                for y in range(4):
                    send1c[step - 1, pl.ds((x * 4 + y) * 32, 32), :] = encode(acc[x, zk, y, 96:128, :], inverse)
            send1c[step - 1, pl.ds(512, 16), :] = exponent
            slab.append(send(send1c.at[step - 1], recv1c.at[step - 1], moved(me, z=step)))
        for d in (2, 1, 3):
            to = (px + d) % 4
            for y in range(4):
                send1a[k, d - 1, pl.ds(y * 48, 48), :] = encode(acc[to, zk, y, 0:48, :], inverse)
            send1a[k, d - 1, pl.ds(192, 16), :] = exponent
            slab.append(send(send1a.at[k, d - 1], recv1a.at[k, d - 1], moved(me, x=d)))
            to = (py + d) % 4
            for x in range(4):
                send1b[k, d - 1, pl.ds(x * 48, 48), :] = encode(acc[x, zk, to, 48:96, :], inverse)
            send1b[k, d - 1, pl.ds(192, 16), :] = exponent
            slab.append(send(send1b.at[k, d - 1], recv1b.at[k, d - 1], moved(me, y=d)))
        sends1.append(slab)

    first_half(0)
    state_copies = swap_state()
    for k in range(4):
        second_half(k)
        if k < 3:
            first_half(k + 1)
        join(k)

    def finish(k):
        step = SLAB_ORDER[k]
        zk = (pz + step) % 4
        slab = list(sends1[k])
        if step:
            slab.pop(0).wait_recv()
            scale = jnp.exp2(splat(recv1c[step - 1, pl.ds(512, 16), :]))
            for x in range(4):
                for y in range(4):
                    acc[x, pz, y, 96:128, :] += scale * recv1c[step - 1, pl.ds((x * 4 + y) * 32, 32), :].astype(F32)
        for n, d in enumerate((2, 1, 3)):
            slab[2 * n].wait_recv()
            scale = jnp.exp2(splat(recv1a[k, d - 1, pl.ds(192, 16), :]))
            for y in range(4):
                acc[px, zk, y, 0:48, :] += scale * recv1a[k, d - 1, pl.ds(y * 48, 48), :].astype(F32)
            slab[2 * n + 1].wait_recv()
            scale = jnp.exp2(splat(recv1b[k, d - 1, pl.ds(192, 16), :]))
            for x in range(4):
                acc[x, zk, py, 48:96, :] += scale * recv1b[k, d - 1, pl.ds(x * 48, 48), :].astype(F32)

    def later_phase(axis, out_buf, in_buf, rows, first, count, place):
        held = [[acc[(*place(j, (me[axis] + d) % 4), pl.ds(first, rows), slice(None))] for j in range(count)] for d in (2, 1, 3)]
        top = functools.reduce(jnp.maximum, [jnp.max(jnp.abs(v).reshape(rows // 8, 8, 128), axis=0) for h in held for v in h])
        exponent = exponent_of(top)
        inverse = jnp.exp2(-exponent)[0:1, :]
        exponent = exponent.astype(jnp.int32).astype(jnp.int16)
        copies = []
        for h, d in zip(held, (2, 1, 3), strict=True):
            for j, v in enumerate(h):
                out_buf[d - 1, pl.ds(j * rows, rows), :] = encode(v, inverse)
            out_buf[d - 1, pl.ds(count * rows, 16), :] = exponent
            copies.append(send(out_buf.at[d - 1], in_buf.at[d - 1], moved(me, **{axis: d})))

        def add():
            for d, copy in zip((2, 1, 3), copies, strict=True):
                copy.wait_recv()
                scale = jnp.exp2(splat(in_buf[d - 1, pl.ds(count * rows, 16), :]))
                for j in range(count):
                    acc[(*place(j, me[axis]), pl.ds(first, rows), slice(None))] += scale * in_buf[d - 1, pl.ds(j * rows, rows), :].astype(F32)

        return add

    for k in range(3):
        finish(k)
    adds = [later_phase("x", send2c, recv2c, 32, 96, 4, lambda j, q: (q, pz, j))]
    finish(3)
    adds += [
        later_phase("y", send2a, recv2a, 48, 0, 4, lambda j, q: (px, j, q)),
        later_phase("z", send2b, recv2b, 48, 48, 4, lambda j, q: (j, q, py)),
    ]
    adds[0]()
    last = [later_phase("y", send3c, recv3c, 32, 96, 1, lambda j, q: (px, pz, q))]
    adds[1]()
    last.append(later_phase("z", send3a, recv3a, 48, 0, 1, lambda j, q: (px, q, py)))
    adds[2]()
    last.append(later_phase("x", send3b, recv3b, 48, 48, 1, lambda j, q: (q, pz, py)))
    counts = live_ref[0:1, :].astype(F32)
    owner = ((px * 4 + pz) * 2 + pc) * 4 + py
    at = lax.broadcasted_iota(jnp.int32, (1, 128), 1)
    mine = jnp.sum(jnp.where(at == owner, counts, 0.0))
    live_total = jnp.sum(counts) * float(SIDE * SIDE)
    slot = 2 * (lax.broadcasted_iota(jnp.int32, (128, 128), 0) // SIDE) + lax.broadcasted_iota(jnp.int32, (128, 128), 1) // SIDE
    live = slot.astype(F32) < mine
    for add in last:
        add()

    own = jnp.where(live, acc[px, pz, py], 0.0)
    sum_send[0] = jnp.full((1, 128), jnp.sum(own * own), F32)
    copies = []
    for n, by in enumerate([{"x": d, "c": c} for d in (2, 1, 3) for c in (1, 0)] + [{"c": 1}]):
        copies.append(send(sum_send.at[0], sum_recv.at[n], moved(me, **by)))
    turned[...] = own.T
    even, odd = turned[pl.ds(0, SIDE, 2), :], turned[pl.ds(1, SIDE, 2), :]
    flat[pl.ds(0, SIDE), :] = jnp.where(lane < SIDE, even, pltpu.roll(odd, SIDE, 1))
    flat[pl.ds(SIDE, SIDE), :] = jnp.where(lane < SIDE, pltpu.roll(even, SIDE, 1), odd)
    for t in range(32):
        to, part = part_of(t)
        swap_send[to, part // 2, pl.ds(4 * (part % 2), 4), :] = flat[pl.ds(t, 4, 32), :]
    swaps = [send(swap_send.at[(py + d) % 4], swap_recv.at[py], moved(me, y=d)) for d in (2, 1, 3)]
    swap_recv[py] = swap_send[py]
    square = sum_send[0]
    for n, copy in enumerate(copies):
        copy.wait_recv()
        square += sum_recv[n]
    sum_send[1] = square
    copies = []
    for i in (2, 1, 3, 0):
        for j in (2, 1, 3, 0):
            if i or j:
                copies.append(send(sum_send.at[1], sum_recv.at[7 + len(copies)], moved(me, y=i, z=j)))
    for n, copy in enumerate(copies):
        copy.wait_recv()
        square += sum_recv[7 + n]
    for copy in swaps + state_copies:
        copy.wait_recv()
    mean_square = square / live_total
    clip = jnp.minimum(1.0, 1.0 / jnp.sqrt(mean_square + 1e-06))

    for part in range(8):
        for source in range(4):
            rows, at = pl.ds(4 * source, 4), pl.ds(4 * (part % 2), 4)
            joined[3, part, rows, :] = swap_recv[source, part // 2, at, :]
            for n in range(3):
                joined[n, part, rows, :] = state_recv[source, n, part // 2, at, :]
    part = 0
    for first, width in GATHER:
        for column in range(0, width, 128):
            at = pl.multiple_of(first + column + py * width, 128)
            new_master, _, _ = adamw(clip[0:1] * joined[3, part], joined[0, part], joined[1, part], joined[2, part])
            held[px, pz, :, pl.ds(at, 128)] = new_master.astype(jnp.bfloat16)
            part += 1

    def spread(n, fixed, axis, steps=(2, 1, 3)):
        part = region(held, n, fixed)
        return {d: send(part, part, moved(me, **{axis: d})) for d in steps}

    orders = [order for _, _, order in STREAMS]
    inner = [spread(n, {"x": px, "y": py, "z": pz}, order[2]) for n, order in enumerate(orders)]
    for t in range(32):
        at = pl.ds(t * 128, 128)
        clipped = clip * flat[pl.ds(t, 4, 32), :]
        new_master, new_moment, new_variance = adamw(clipped, master_ref[:, at], moment_ref[:, at], variance_ref[:, at])
        clipped_ref[:, at] = clipped
        new_moment_ref[:, at] = new_moment
        new_variance_ref[:, at] = new_variance
        new_master_ref[:, at] = new_master
    stores = []

    def store(src, dst):
        copy = pltpu.make_async_copy(src, dst, store_sem.at[len(stores)])
        copy.start()
        stores.append(copy)

    store(new_master_ref, new_master_hbm)
    store(new_moment_ref, new_moment_hbm)
    store(new_variance_ref, new_variance_hbm)
    store(clipped_ref, clipped_hbm)
    middle = []
    for n, order in enumerate(orders):
        for copy in inner[n].values():
            copy.wait_recv()
        middle.append(spread(n, {a: me[a] for a in order[:2]}, order[1]))
    turns = (0, 1, 3, 2)
    outer, beyond = [[] for _ in orders], [{} for _ in orders]

    def outward(m):
        for n, order in enumerate(orders):
            if m:
                middle[n][turns[m]].wait_recv()
            fixed = {order[0]: me[order[0]], order[1]: (me[order[1]] - turns[m]) % 4}
            outer[n].append(spread(n, fixed, order[0], (1, 3)))

    def onward(m):
        d = 1 if m < 2 else 3
        for n, order in enumerate(orders):
            outer[n][m].pop(d).wait_recv()
            fixed = {order[0]: (me[order[0]] - d) % 4, order[1]: (me[order[1]] - turns[m]) % 4}
            beyond[n].update({m: spread(n, fixed, order[0], (d,))[d]})

    outward(0)
    outward(1)
    onward(0)
    outward(2)
    outward(3)
    for m in (1, 2, 3):
        onward(m)
    other = moved(me, c=1)
    passed = []

    def settle(n, fixed):
        part, place = region(held, n, fixed), region(published, n, fixed, pc)
        passed.append(send(part, place, other))
        store(part, place)

    for n, order in enumerate(orders):
        settle(n, {order[0]: me[order[0]]})
    for d in (1, 3):
        for n, order in enumerate(orders):
            for piece in outer[n]:
                if d in piece:
                    piece[d].wait_recv()
            settle(n, {order[0]: (me[order[0]] - d) % 4})
    for m in range(4):
        for n, order in enumerate(orders):
            beyond[n][m].wait_recv()
            settle(n, {order[0]: (me[order[0]] - 2) % 4, order[1]: (me[order[1]] - turns[m]) % 4})
    for copy in passed:
        copy.wait_recv()
    for copy in issued:
        copy.wait_send()
    for copy in stores:
        copy.wait()


def pass_on(*refs):
    sources, results, sem = refs[:5], refs[5:10], refs[10]
    copies = []
    for i in range(4):
        rows = pl.ds(i * 128, 128)
        copies.append(pltpu.make_async_copy(sources[4].at[rows], results[4].at[rows], sem.at[i]))
        copies.append(pltpu.make_async_copy(sources[i], results[i], sem.at[4 + i]))
    for copy in copies:
        copy.start()
    for copy in copies:
        copy.wait()


def local(hidden, grad_out, block_list, live_block_count, master, moment, variance):
    i16 = jnp.int16
    state = jax.ShapeDtypeStruct(master.shape, F32)
    vmem, hbm = pl.BlockSpec(memory_space=pltpu.VMEM), pl.BlockSpec(memory_space=pltpu.HBM)
    first = [pltpu.VMEM((4, 3, 208, 128), i16)] * 4 + [pltpu.VMEM((3, 528, 128), i16)] * 2
    second = [pltpu.VMEM((3, 208, 128), i16)] * 4 + [pltpu.VMEM((3, 144, 128), i16)] * 2
    third = [pltpu.VMEM((3, 64, 128), i16)] * 4 + [pltpu.VMEM((3, 48, 128), i16)] * 2
    copies = 4 + 27 + 18 + 22 + 3 + 3 + 9 + 9 + 36 + 21
    *updated, published = pl.pallas_call(
        kernel,
        out_shape=[state] * 4 + [jax.ShapeDtypeStruct((4, 4, 2, 16, 4096), jnp.bfloat16)],
        in_specs=[hbm] * 7,
        out_specs=[hbm] * 5,
        scratch_shapes=[
            pltpu.SMEM(block_list.shape[::-1], jnp.int32),
            pltpu.VMEM(hidden.shape, jnp.bfloat16),
            pltpu.VMEM(grad_out.shape, jnp.bfloat16),
            pltpu.VMEM(grad_out.shape[::-1], jnp.bfloat16),
            pltpu.VMEM((1, live_block_count.shape[0]), jnp.int32),
            *[pltpu.VMEM(master.shape, F32)] * 7,
            pltpu.VMEM((4, 4, 4, 128, 128), F32),
            pltpu.VMEM((4, 4, 128, 128), F32),
            pltpu.VMEM((4, 2064, 128), i16),
            pltpu.VMEM((4, 2064, 128), i16),
            *first, *second, *third,
            pltpu.VMEM((128, 128), F32),
            pltpu.VMEM((128, 128), F32),
            pltpu.VMEM((2, 1, 128), F32),
            pltpu.VMEM((22, 1, 128), F32),
            pltpu.VMEM((4, 4, 8, 128), F32),
            pltpu.VMEM((4, 4, 8, 128), F32),
            pltpu.VMEM((4, 3, 4, 8, 128), F32),
            pltpu.VMEM((4, 3, 4, 8, 128), F32),
            pltpu.VMEM((4, 8, 16, 128), F32),
            pltpu.VMEM((4, 4, 16, 4096), jnp.bfloat16),
            pltpu.SemaphoreType.DMA((11,)),
            pltpu.SemaphoreType.DMA((25,)),
            pltpu.SemaphoreType.DMA((copies,)),
            pltpu.SemaphoreType.DMA((copies,)),
        ],
        compiler_params=pltpu.CompilerParams(
            collective_id=0, has_side_effects=True, vmem_limit_bytes=30 * 2**20
        ),
    )(
        *[pltpu.with_memory_space_constraint(a, pltpu.HBM) for a in (block_list.T, hidden, grad_out, live_block_count.reshape(1, -1), master, moment, variance)],
    )
    return pl.pallas_call(
        pass_on,
        out_shape=[state] * 4 + [jax.ShapeDtypeStruct((512, 4096), jnp.bfloat16)],
        in_specs=[hbm] * 5,
        out_specs=[hbm] * 5,
        scratch_shapes=[pltpu.SemaphoreType.DMA((8,))],
        compiler_params=pltpu.CompilerParams(vmem_limit_bytes=2**20),
    )(*updated, published.reshape(512, 4096))


def solution(mesh):
    one, all_of_it = P(("dp", "owner"), None), P()
    return jax.shard_map(
        local,
        mesh=mesh,
        in_specs=(one, one, all_of_it, all_of_it, one, one, one),
        out_specs=(one, one, one, one, all_of_it),
        check_vma=False,
    )
```

```python
import functools

import jax
import jax.numpy as jnp
from jax import lax
from jax.experimental import pallas as pl
from jax.experimental.pallas import tpu as pltpu
from jax.sharding import PartitionSpec as P

MESH = pl.DeviceIdType.MESH
SIDE = 64
UNROLL = 32
SLAB_ORDER = (2, 1, 3, 0)
STREAMS = ((0, 48, "xyz"), (48, 48, "yzx"), (96, 32, "zxy"))
F32 = jnp.float32


def where_am_i():
    dp = lax.axis_index("dp")
    y = lax.axis_index("owner")
    return {"x": dp // 8, "z": (dp // 2) % 4, "c": dp % 2, "y": y}


def device_at(place):
    return ((place["x"] * 4 + place["z"]) * 2 + place["c"], place["y"])


def moved(me, **by):
    place = dict(me)
    for axis, step in by.items():
        place[axis] = (me[axis] + step) % (2 if axis == "c" else 4)
    return place


def exponent_of(top):
    top = jnp.maximum(jnp.full((16, 128), jnp.max(top), F32), 1e-30)
    return jnp.ceil(jnp.log2(top * (1.0 / 32000.0)))


def encode(values, inverse):
    return jnp.round(values * inverse).astype(jnp.int32).astype(jnp.int16)


def splat(tile):
    return tile[0:1, :].astype(F32)


GATHER = ((0, 384), (1536, 384), (3072, 256))


def region(buf, n, fixed, core=None):
    first, width = GATHER[n]
    start, size = (first + fixed["y"] * width, width) if "y" in fixed else (first, 4 * width)
    index = [fixed.get(a, slice(None)) for a in "xz"] + ([] if core is None else [core])
    return buf.at[(*index, slice(None), pl.ds(start, size))]


def part_of(t):
    to, part = divmod(t, 3) if t < 12 else divmod(t - 12, 3) if t < 24 else divmod(t - 24, 2)
    return to, part + (0 if t < 12 else 3 if t < 24 else 6)


def adamw(clipped, master, moment, variance):
    new_moment = 0.9 * moment + 0.1 * clipped
    new_variance = 0.95 * variance + 0.05 * clipped * clipped
    moment_hat = new_moment / (1.0 - 0.9**20)
    variance_hat = new_variance / (1.0 - 0.95**20)
    new_master = master - 0.02 * (moment_hat / (jnp.sqrt(variance_hat) + 1e-08) + 0.1 * master)
    return new_master, new_moment, new_variance


def kernel(
    list_hbm, hidden_hbm, grad_out_hbm, live_hbm, master_hbm, moment_hbm, variance_hbm,
    new_master_hbm, new_moment_hbm, new_variance_hbm, clipped_hbm, published,
    list_ref, hidden, grad_out, grad_out_t, live_ref, master_ref, moment_ref, variance_ref,
    new_master_ref, new_moment_ref, new_variance_ref, clipped_ref, acc, pair_part, sib_send, sib_recv,
    send1a, recv1a, send1b, recv1b, send1c, recv1c,
    send2a, recv2a, send2b, recv2b, send2c, recv2c,
    send3a, recv3a, send3b, recv3b, send3c, recv3c,
    turned, flat, sum_send, sum_recv, swap_send, swap_recv, state_send, state_recv, joined, held,
    load_sem, store_sem, send_sem, recv_sem,
):
    me = where_am_i()
    px, py, pz, pc = me["x"], me["y"], me["z"], me["c"]
    peers = [moved(me, c=1)]
    peers += [moved(me, **{a: d}) for a in "xyz" for d in (1, 2, 3)]
    peers += [moved(me, x=d, c=1) for d in (1, 2, 3)]
    peers += [moved(me, y=i, z=j) for i in (1, 2, 3) for j in (1, 2, 3)]
    barrier = pltpu.get_barrier_semaphore()
    for peer in peers:
        pl.semaphore_signal(barrier, inc=1, device_id=device_at(peer), device_id_type=MESH)

    loads = [
        pltpu.make_async_copy(grad_out_hbm, grad_out, load_sem.at[0]),
        pltpu.make_async_copy(hidden_hbm, hidden, load_sem.at[1]),
        pltpu.make_async_copy(list_hbm, list_ref, load_sem.at[6]),
        pltpu.make_async_copy(live_hbm, live_ref, load_sem.at[2]),
        pltpu.make_async_copy(master_hbm, master_ref, load_sem.at[3]),
        pltpu.make_async_copy(moment_hbm, moment_ref, load_sem.at[4]),
        pltpu.make_async_copy(variance_hbm, variance_ref, load_sem.at[5]),
    ]
    for load in loads:
        load.start()

    loads[0].wait()
    for t in range(20):
        grad_out_t[pl.ds(t * 128, 128), :] = grad_out[:, t * 128 : (t + 1) * 128].T
    loads[1].wait()
    loads[2].wait()
    pl.semaphore_wait(barrier, len(peers))

    issued = []

    def send(src, dst, to):
        n = len(issued)
        copy = pltpu.make_async_remote_copy(
            src_ref=src, dst_ref=dst, send_sem=send_sem.at[n], recv_sem=recv_sem.at[n],
            device_id=device_at(to), device_id_type=MESH,
        )
        copy.start()
        issued.append(copy)
        return copy

    lane = lax.broadcasted_iota(jnp.int32, (SIDE, 128), 1)

    low = lane < SIDE

    def two_blocks(pair):
        both, odd = [], []
        for slot in (2 * pair, 2 * pair + 1):
            row, column = list_ref[0, slot], list_ref[1, slot]
            left = grad_out_t[pl.ds(column * SIDE, SIDE), :]
            right = hidden[:, pl.ds((row >> 1) * 128, 128)]
            both.append(jnp.dot(left, right, preferred_element_type=F32))
            odd.append(row & 1)
        crossed = pltpu.roll(jnp.where(low, both[1], both[0]), SIDE, 1)
        straight = jnp.where(low, both[0], both[1])
        return jnp.where(jnp.where(low, odd[0], 1 - odd[1]) == 1, crossed, straight)

    def swap_state():
        for load in loads[3:]:
            load.wait()
        for n, ref in enumerate((master_ref, moment_ref, variance_ref)):
            for t in range(32):
                to, part = part_of(t)
                state_send[to, n, part // 2, pl.ds(4 * (part % 2), 4), :] = ref[:, t * 128 : (t + 1) * 128]
        state_recv[py] = state_send[py]
        return [send(state_send.at[(py + d) % 4], state_recv.at[py], moved(me, y=d)) for d in (2, 1, 3)]

    sends1, to_sibling = [], []

    def first_half(k):
        zk = (pz + SLAB_ORDER[k]) % 4

        def for_sibling(i, top):
            for u in range(UNROLL):
                n = UNROLL * i + u
                x, y, p = n // 8, (n // 2) % 4, n % 2
                owner = ((x * 4 + zk) * 2 + (1 - pc)) * 4 + y
                part = two_blocks(2 * owner + p)
                pair_part[x, y, pl.ds(p * SIDE, SIDE), :] = part
                top = jnp.maximum(top, jnp.max(jnp.abs(part).reshape(8, 8, 128), axis=0))
            return top

        top = lax.fori_loop(0, 32 // UNROLL, for_sibling, jnp.zeros((8, 128), F32))
        exponent = exponent_of(top)
        inverse = jnp.exp2(-exponent)[0:1, :]
        for x in range(4):
            for y in range(4):
                sib_send[k, pl.ds((x * 4 + y) * 128, 128), :] = encode(pair_part[x, y], inverse)
        sib_send[k, pl.ds(2048, 16), :] = exponent.astype(jnp.int32).astype(jnp.int16)
        to_sibling.append(send(sib_send.at[k], sib_recv.at[k], moved(me, c=1)))

    def second_half(k):
        zk = (pz + SLAB_ORDER[k]) % 4

        def for_self(i, carry):
            for u in range(UNROLL):
                n = UNROLL * i + u
                x, y, p = n // 8, (n // 2) % 4, n % 2
                owner = ((x * 4 + zk) * 2 + pc) * 4 + y
                acc[x, zk, y, pl.ds(p * SIDE, SIDE), :] = two_blocks(2 * owner + p)
            return carry

        lax.fori_loop(0, 32 // UNROLL, for_self, 0)

    def join(k):
        step = SLAB_ORDER[k]
        zk = (pz + step) % 4
        to_sibling[k].wait_recv()
        scale = jnp.exp2(splat(sib_recv[k, pl.ds(2048, 16), :]))
        top = jnp.zeros((8, 128), F32)
        for x in range(4):
            for y in range(4):
                total = acc[x, zk, y] + scale * sib_recv[k, pl.ds((x * 4 + y) * 128, 128), :].astype(F32)
                acc[x, zk, y] = total
                top = jnp.maximum(top, jnp.max(jnp.abs(total).reshape(16, 8, 128), axis=0))
        exponent = exponent_of(top)
        inverse = jnp.exp2(-exponent)[0:1, :]
        exponent = exponent.astype(jnp.int32).astype(jnp.int16)
        slab = []
        if step:
            for x in range(4):
                for y in range(4):
                    send1c[step - 1, pl.ds((x * 4 + y) * 32, 32), :] = encode(acc[x, zk, y, 96:128, :], inverse)
            send1c[step - 1, pl.ds(512, 16), :] = exponent
            slab.append(send(send1c.at[step - 1], recv1c.at[step - 1], moved(me, z=step)))
        for d in (2, 1, 3):
            to = (px + d) % 4
            for y in range(4):
                send1a[k, d - 1, pl.ds(y * 48, 48), :] = encode(acc[to, zk, y, 0:48, :], inverse)
            send1a[k, d - 1, pl.ds(192, 16), :] = exponent
            slab.append(send(send1a.at[k, d - 1], recv1a.at[k, d - 1], moved(me, x=d)))
            to = (py + d) % 4
            for x in range(4):
                send1b[k, d - 1, pl.ds(x * 48, 48), :] = encode(acc[x, zk, to, 48:96, :], inverse)
            send1b[k, d - 1, pl.ds(192, 16), :] = exponent
            slab.append(send(send1b.at[k, d - 1], recv1b.at[k, d - 1], moved(me, y=d)))
        sends1.append(slab)

    first_half(0)
    state_copies = swap_state()
    for k in range(4):
        second_half(k)
        if k < 3:
            first_half(k + 1)
        join(k)

    def finish(k):
        step = SLAB_ORDER[k]
        zk = (pz + step) % 4
        slab = list(sends1[k])
        if step:
            slab.pop(0).wait_recv()
            scale = jnp.exp2(splat(recv1c[step - 1, pl.ds(512, 16), :]))
            for x in range(4):
                for y in range(4):
                    acc[x, pz, y, 96:128, :] += scale * recv1c[step - 1, pl.ds((x * 4 + y) * 32, 32), :].astype(F32)
        for n, d in enumerate((2, 1, 3)):
            slab[2 * n].wait_recv()
            scale = jnp.exp2(splat(recv1a[k, d - 1, pl.ds(192, 16), :]))
            for y in range(4):
                acc[px, zk, y, 0:48, :] += scale * recv1a[k, d - 1, pl.ds(y * 48, 48), :].astype(F32)
            slab[2 * n + 1].wait_recv()
            scale = jnp.exp2(splat(recv1b[k, d - 1, pl.ds(192, 16), :]))
            for x in range(4):
                acc[x, zk, py, 48:96, :] += scale * recv1b[k, d - 1, pl.ds(x * 48, 48), :].astype(F32)

    for k in range(4):
        finish(k)

    def later_phase(axis, out_buf, in_buf, rows, first, count, place):
        held = [[acc[(*place(j, (me[axis] + d) % 4), pl.ds(first, rows), slice(None))] for j in range(count)] for d in (2, 1, 3)]
        top = functools.reduce(jnp.maximum, [jnp.max(jnp.abs(v).reshape(rows // 8, 8, 128), axis=0) for h in held for v in h])
        exponent = exponent_of(top)
        inverse = jnp.exp2(-exponent)[0:1, :]
        exponent = exponent.astype(jnp.int32).astype(jnp.int16)
        copies = []
        for h, d in zip(held, (2, 1, 3), strict=True):
            for j, v in enumerate(h):
                out_buf[d - 1, pl.ds(j * rows, rows), :] = encode(v, inverse)
            out_buf[d - 1, pl.ds(count * rows, 16), :] = exponent
            copies.append(send(out_buf.at[d - 1], in_buf.at[d - 1], moved(me, **{axis: d})))

        def add():
            for d, copy in zip((2, 1, 3), copies, strict=True):
                copy.wait_recv()
                scale = jnp.exp2(splat(in_buf[d - 1, pl.ds(count * rows, 16), :]))
                for j in range(count):
                    acc[(*place(j, me[axis]), pl.ds(first, rows), slice(None))] += scale * in_buf[d - 1, pl.ds(j * rows, rows), :].astype(F32)

        return add

    adds = [
        later_phase("x", send2c, recv2c, 32, 96, 4, lambda j, q: (q, pz, j)),
        later_phase("y", send2a, recv2a, 48, 0, 4, lambda j, q: (px, j, q)),
        later_phase("z", send2b, recv2b, 48, 48, 4, lambda j, q: (j, q, py)),
    ]
    adds[0]()
    last = [later_phase("y", send3c, recv3c, 32, 96, 1, lambda j, q: (px, pz, q))]
    adds[1]()
    last.append(later_phase("z", send3a, recv3a, 48, 0, 1, lambda j, q: (px, q, py)))
    adds[2]()
    last.append(later_phase("x", send3b, recv3b, 48, 48, 1, lambda j, q: (q, pz, py)))
    counts = live_ref[0:1, :].astype(F32)
    owner = ((px * 4 + pz) * 2 + pc) * 4 + py
    at = lax.broadcasted_iota(jnp.int32, (1, 128), 1)
    mine = jnp.sum(jnp.where(at == owner, counts, 0.0))
    live_total = jnp.sum(counts) * float(SIDE * SIDE)
    slot = 2 * (lax.broadcasted_iota(jnp.int32, (128, 128), 0) // SIDE) + lax.broadcasted_iota(jnp.int32, (128, 128), 1) // SIDE
    live = slot.astype(F32) < mine
    for add in last:
        add()

    own = jnp.where(live, acc[px, pz, py], 0.0)
    sum_send[0] = jnp.full((1, 128), jnp.sum(own * own), F32)
    copies = []
    for n, by in enumerate([{"c": 1}] + [{"x": d, "c": c} for d in (1, 2, 3) for c in (0, 1)]):
        copies.append(send(sum_send.at[0], sum_recv.at[n], moved(me, **by)))
    turned[...] = own.T
    even, odd = turned[pl.ds(0, SIDE, 2), :], turned[pl.ds(1, SIDE, 2), :]
    flat[pl.ds(0, SIDE), :] = jnp.where(lane < SIDE, even, pltpu.roll(odd, SIDE, 1))
    flat[pl.ds(SIDE, SIDE), :] = jnp.where(lane < SIDE, pltpu.roll(even, SIDE, 1), odd)
    for t in range(32):
        to, part = part_of(t)
        swap_send[to, part // 2, pl.ds(4 * (part % 2), 4), :] = flat[pl.ds(t, 4, 32), :]
    swaps = [send(swap_send.at[(py + d) % 4], swap_recv.at[py], moved(me, y=d)) for d in (2, 1, 3)]
    swap_recv[py] = swap_send[py]
    square = sum_send[0]
    for n, copy in enumerate(copies):
        copy.wait_recv()
        square += sum_recv[n]
    sum_send[1] = square
    copies = []
    for i in range(4):
        for j in range(4):
            if i or j:
                copies.append(send(sum_send.at[1], sum_recv.at[7 + len(copies)], moved(me, y=i, z=j)))
    for n, copy in enumerate(copies):
        copy.wait_recv()
        square += sum_recv[7 + n]
    for copy in swaps + state_copies:
        copy.wait_recv()
    mean_square = square / live_total
    clip = jnp.minimum(1.0, 1.0 / jnp.sqrt(mean_square + 1e-06))

    for part in range(8):
        for source in range(4):
            rows, at = pl.ds(4 * source, 4), pl.ds(4 * (part % 2), 4)
            joined[3, part, rows, :] = swap_recv[source, part // 2, at, :]
            for n in range(3):
                joined[n, part, rows, :] = state_recv[source, n, part // 2, at, :]
    part = 0
    for first, width in GATHER:
        for column in range(0, width, 128):
            at = pl.multiple_of(first + column + py * width, 128)
            new_master, _, _ = adamw(clip[0:1] * joined[3, part], joined[0, part], joined[1, part], joined[2, part])
            held[px, pz, :, pl.ds(at, 128)] = new_master.astype(jnp.bfloat16)
            part += 1

    def spread(n, fixed, axis, steps=(2, 1, 3)):
        part = region(held, n, fixed)
        return {d: send(part, part, moved(me, **{axis: d})) for d in steps}

    orders = [order for _, _, order in STREAMS]
    inner = [spread(n, {"x": px, "y": py, "z": pz}, order[2]) for n, order in enumerate(orders)]
    for t in range(32):
        at = pl.ds(t * 128, 128)
        clipped = clip * flat[pl.ds(t, 4, 32), :]
        new_master, new_moment, new_variance = adamw(clipped, master_ref[:, at], moment_ref[:, at], variance_ref[:, at])
        clipped_ref[:, at] = clipped
        new_moment_ref[:, at] = new_moment
        new_variance_ref[:, at] = new_variance
        new_master_ref[:, at] = new_master
    stores = []

    def store(src, dst):
        copy = pltpu.make_async_copy(src, dst, store_sem.at[len(stores)])
        copy.start()
        stores.append(copy)

    store(new_master_ref, new_master_hbm)
    store(new_moment_ref, new_moment_hbm)
    store(new_variance_ref, new_variance_hbm)
    store(clipped_ref, clipped_hbm)
    middle = []
    for n, order in enumerate(orders):
        for copy in inner[n].values():
            copy.wait_recv()
        middle.append(spread(n, {a: me[a] for a in order[:2]}, order[1]))
    turns = (0, 1, 3, 2)
    outer, beyond = [[] for _ in orders], [{} for _ in orders]

    def outward(m):
        for n, order in enumerate(orders):
            if m:
                middle[n][turns[m]].wait_recv()
            fixed = {order[0]: me[order[0]], order[1]: (me[order[1]] - turns[m]) % 4}
            outer[n].append(spread(n, fixed, order[0], (1, 3)))

    def onward(m):
        d = 1 if m < 2 else 3
        for n, order in enumerate(orders):
            outer[n][m].pop(d).wait_recv()
            fixed = {order[0]: (me[order[0]] - d) % 4, order[1]: (me[order[1]] - turns[m]) % 4}
            beyond[n].update({m: spread(n, fixed, order[0], (d,))[d]})

    other = moved(me, c=1)
    passed = []

    def settle(n, fixed):
        part, place = region(held, n, fixed), region(published, n, fixed, pc)
        passed.append(send(part, place, other))
        store(part, place)

    outward(0)
    outward(1)
    onward(0)
    outward(2)
    outward(3)
    onward(1)
    for n, order in enumerate(orders):
        settle(n, {order[0]: me[order[0]]})
    for m in (2, 3):
        onward(m)
    for d in (1, 3):
        for n, order in enumerate(orders):
            for piece in outer[n]:
                if d in piece:
                    piece[d].wait_recv()
            settle(n, {order[0]: (me[order[0]] - d) % 4})
    for m in range(4):
        for n, order in enumerate(orders):
            beyond[n][m].wait_recv()
            settle(n, {order[0]: (me[order[0]] - 2) % 4, order[1]: (me[order[1]] - turns[m]) % 4})
    for copy in passed:
        copy.wait_recv()
    for copy in issued:
        copy.wait_send()
    for copy in stores:
        copy.wait()


def pass_on(*refs):
    sources, results, sem = refs[:5], refs[5:10], refs[10]
    copies = []
    for i in range(4):
        rows = pl.ds(i * 128, 128)
        copies.append(pltpu.make_async_copy(sources[4].at[rows], results[4].at[rows], sem.at[i]))
        copies.append(pltpu.make_async_copy(sources[i], results[i], sem.at[4 + i]))
    for copy in copies:
        copy.start()
    for copy in copies:
        copy.wait()


def local(hidden, grad_out, block_list, live_block_count, master, moment, variance):
    i16 = jnp.int16
    state = jax.ShapeDtypeStruct(master.shape, F32)
    vmem, hbm = pl.BlockSpec(memory_space=pltpu.VMEM), pl.BlockSpec(memory_space=pltpu.HBM)
    first = [pltpu.VMEM((4, 3, 208, 128), i16)] * 4 + [pltpu.VMEM((3, 528, 128), i16)] * 2
    second = [pltpu.VMEM((3, 208, 128), i16)] * 4 + [pltpu.VMEM((3, 144, 128), i16)] * 2
    third = [pltpu.VMEM((3, 64, 128), i16)] * 4 + [pltpu.VMEM((3, 48, 128), i16)] * 2
    copies = 4 + 27 + 18 + 22 + 3 + 3 + 9 + 9 + 36 + 21
    *updated, published = pl.pallas_call(
        kernel,
        out_shape=[state] * 4 + [jax.ShapeDtypeStruct((4, 4, 2, 16, 4096), jnp.bfloat16)],
        in_specs=[hbm] * 7,
        out_specs=[hbm] * 5,
        scratch_shapes=[
            pltpu.SMEM(block_list.shape[::-1], jnp.int32),
            pltpu.VMEM(hidden.shape, jnp.bfloat16),
            pltpu.VMEM(grad_out.shape, jnp.bfloat16),
            pltpu.VMEM(grad_out.shape[::-1], jnp.bfloat16),
            pltpu.VMEM((1, live_block_count.shape[0]), jnp.int32),
            *[pltpu.VMEM(master.shape, F32)] * 7,
            pltpu.VMEM((4, 4, 4, 128, 128), F32),
            pltpu.VMEM((4, 4, 128, 128), F32),
            pltpu.VMEM((4, 2064, 128), i16),
            pltpu.VMEM((4, 2064, 128), i16),
            *first, *second, *third,
            pltpu.VMEM((128, 128), F32),
            pltpu.VMEM((128, 128), F32),
            pltpu.VMEM((2, 1, 128), F32),
            pltpu.VMEM((22, 1, 128), F32),
            pltpu.VMEM((4, 4, 8, 128), F32),
            pltpu.VMEM((4, 4, 8, 128), F32),
            pltpu.VMEM((4, 3, 4, 8, 128), F32),
            pltpu.VMEM((4, 3, 4, 8, 128), F32),
            pltpu.VMEM((4, 8, 16, 128), F32),
            pltpu.VMEM((4, 4, 16, 4096), jnp.bfloat16),
            pltpu.SemaphoreType.DMA((7,)),
            pltpu.SemaphoreType.DMA((25,)),
            pltpu.SemaphoreType.DMA((copies,)),
            pltpu.SemaphoreType.DMA((copies,)),
        ],
        compiler_params=pltpu.CompilerParams(
            collective_id=0, has_side_effects=True, vmem_limit_bytes=30 * 2**20
        ),
    )(
        *[pltpu.with_memory_space_constraint(a, pltpu.HBM) for a in (block_list.T, hidden, grad_out, live_block_count.reshape(1, -1), master, moment, variance)],
    )
    return pl.pallas_call(
        pass_on,
        out_shape=[state] * 4 + [jax.ShapeDtypeStruct((512, 4096), jnp.bfloat16)],
        in_specs=[hbm] * 5,
        out_specs=[hbm] * 5,
        scratch_shapes=[pltpu.SemaphoreType.DMA((8,))],
        compiler_params=pltpu.CompilerParams(vmem_limit_bytes=2**20),
    )(*updated, published.reshape(512, 4096))


def solution(mesh):
    one, all_of_it = P(("dp", "owner"), None), P()
    return jax.shard_map(
        local,
        mesh=mesh,
        in_specs=(one, one, all_of_it, all_of_it, one, one, one),
        out_specs=(one, one, one, one, all_of_it),
        check_vma=False,
    )
```
